32 devices in a mesh: groups: 2 (over x), cache: 8 (over z, y), tensor: 2 (over core).
Axes of the slice: x: 2, y: 2, z: 4, core: 2. Of those that a mesh axis runs over, the one named last changes fastest.
Arguments:
- x_in: bfloat16 [8192, 4096], P(('groups', 'cache'), 'tensor'), parts along dimension 0, may hold values from -6 to 6
- z_in: bfloat16 [8192, 4096], P(('groups', 'cache'), 'tensor'), parts along dimension 0, may hold values from -6 to 6
- bc_in: bfloat16 [8192, 512], P(('groups', 'cache')), parts along dimension 0, may hold values from -6 to 6
- dt_in: float32 [8192, 64], P(('groups', 'cache'), 'tensor'), parts along dimension 0, may hold values from -3 to 43
- conv_x: bfloat16 [4, 4096], P(None, 'tensor'), may hold values from -3 to 3
- conv_bc: bfloat16 [4, 512], replicated, may hold values from -3 to 3
- a_log: float32 [64], P('tensor'), may hold values from -8.2 to -2.8
- dt_bias: float32 [64], P('tensor'), may hold values from -1 to 1
- d_skip: float32 [64], P('tensor'), may hold values from 0.02 to 16
- norm_gain: float32 [4096], P('tensor'), may hold values from 0.25 to 1.75
- out_weight: bfloat16 [2560, 4096], P('cache', 'tensor'), may hold values from -0.09375 to 0.09375
- store_ssm: float32 [16, 64, 64, 256], P(('groups', 'cache'), 'tensor'), parts along dimension 0, may hold values from -6 to 6
- stored_conv_inputs: float32 [16, 3, 4096], P(('groups', 'cache'), None, 'tensor'), parts along dimension 0, may hold values from -6 to 6
- store_convbc: float32 [16, 3, 512], P(('groups', 'cache')), parts along dimension 0, may hold values from -6 to 6
- hits: int32 [16, 2], P('groups'), parts along dimension 0, may hold values from 0 to 7, as said below
- assign: int32 [16], P('groups'), parts along dimension 0, may hold values from 0 to 7, each once
- lengths: int32 [16], P(('groups', 'cache')), parts along dimension 0, may hold values from 128 to 512, as said below
Outputs:
- mixed: bfloat16 [8192, 2560], P(('groups', 'cache'), 'tensor'), parts along dimension 0
The draws below stay inside these ranges and needn't reach their ends.
There are 2 independent parts, one for each index of `groups`. The reference program is written for one: setup_inputs(seed, part) draws one part's arguments, and reference() takes and returns one part's arrays. A program takes and returns all parts, laid end to end along the dimension named above; an argument that names none is the same for every part. Nothing has to cross between parts.
Inputs may be any that keep to these rules, and one draw needn't show every extreme that they name: hits[r, 0] is the cache index of the device that stores request r's prefix state and hits[r, 1] its slot there, below 1. No cache index stores the states of more than 4 requests, and one stores exactly 4. Several requests may name the same slot. `assign`: each request appears at exactly one position. `lengths`: one position has all 512 tokens valid.
All inputs are finite; a program needn't handle non-finite values.
Results may differ from the reference program's by a relative error of at most 0.0057.
Values may be sent and summed in bfloat16 or wider, within the bound.
No kernel may reach another device: no remote copies, remote signals or barrier semaphores. Data moves between devices by JAX's collectives and lax.ppermute only.
A program may use at most 128 MiB of HBM per device.

```python
import jax
import jax.numpy as jnp
from jax import lax

HEADS = 64
P_SIZE = 64
NS = 256
D = 2560
KCONV = 4
BLOCK = 128
L = 512
REQ_DEV = 1
SLOTS = 1
REQUESTS = 8
TOKENS = 4096
INNER = 4096
STORE = 8
MOST = 4


def draw_dt_in(key, part):
    key = jax.random.fold_in(key, 21)
    first, latter_portion, third = jax.random.split(key, 3)
    tensor_extent = (TOKENS, HEADS)
    starting_position = jnp.clip(0.5 * jax.random.normal(first, tensor_extent, jnp.float32), -3.0, 3.0)
    transfer_batch = (jax.random.randint(latter_portion, tensor_extent, 0, 128) == 0).astype(jnp.float32)
    lines_per_tile = jax.random.uniform(third, tensor_extent, jnp.float32, 20.0, 40.0)
    return starting_position + transfer_batch * lines_per_tile


def draw_a_log(key, part):
    key = jax.random.fold_in(key, 22)
    lower, upper = (0.001, 0.06)
    spread = jax.random.uniform(key, (HEADS,), jnp.float32)
    return jnp.log(lower) + spread * (jnp.log(upper) - jnp.log(lower))


def draw_d_skip(key, part):
    key = jax.random.fold_in(key, 25)
    lower, upper = (0.1, 4.0)
    spread = jax.random.uniform(key, (HEADS,), jnp.float32)
    return jnp.exp(jnp.log(lower) + spread * (jnp.log(upper) - jnp.log(lower)))


def draw_hits(key, part):
    key = jax.random.fold_in(key, 23)
    first, latter_portion, third = jax.random.split(key, 3)
    devices_here = REQUESTS // REQ_DEV
    order = jax.random.permutation(first, devices_here)
    others = jnp.arange(REQUESTS - MOST) % (devices_here - 1) + 1
    owners = jnp.concatenate([jnp.full((MOST,), order[0], jnp.int32), order[others].astype(jnp.int32)])
    owners = jax.random.permutation(latter_portion, owners)
    slot_ids = jax.random.randint(third, (REQUESTS,), 0, SLOTS)
    return jnp.stack([owners, slot_ids], axis=1).astype(jnp.int32)


def draw_lengths(key, part):
    key = jax.random.fold_in(key, 24)
    first, latter_portion = jax.random.split(key)
    values = jax.random.randint(first, (REQUESTS,), L // 4, L + 1)
    fullest = jax.random.randint(latter_portion, (), 0, REQUESTS)
    return jnp.where(jnp.arange(REQUESTS) == fullest, L, values).astype(jnp.int32)


def level_of(key, dims, cuts, low, top_value):
    factor_of = 1.0
    for axis_at, blocks in cuts:
        draws = jax.random.uniform(jax.random.fold_in(jax.random.fold_in(key, 6), axis_at), (blocks,), jnp.float32, low / len(cuts), top_value / len(cuts))
        factor_of = factor_of * jnp.repeat(jnp.exp(draws), dims[axis_at] // blocks).reshape((-1,) + (1,) * (len(dims) - 1 - axis_at))
    return factor_of


def centred(stream_key, shape, scale, bound, cuts=(), dtype=jnp.bfloat16):
    result = jax.random.normal(stream_key, shape, jnp.float32) * scale
    if len(cuts) > 0:
        result = level_of(stream_key, shape, cuts, -0.22, 0.18) * result
    return jnp.clip(result, min=-bound, max=bound).astype(dtype)


def setup_inputs(seed: int = 0, part: int = 0) -> dict:
    streams_of = jax.random.split(jax.random.key(seed), 18)
    part_keys = jax.random.split(jax.random.fold_in(streams_of[17], part), 18)
    return {
        "x_in": centred(part_keys[0], (TOKENS, INNER), 1.0, 6.0, ((0, 8), (1, 2))),
        "z_in": centred(part_keys[1], (TOKENS, INNER), 1.0, 6.0, ((0, 8), (1, 2))),
        "bc_in": centred(part_keys[2], (TOKENS, 2 * NS), 1.0, 6.0, ((0, 8),)),
        "dt_in": draw_dt_in(jax.random.fold_in(jax.random.fold_in(streams_of[17], part), 71), part),
        "conv_x": centred(streams_of[4], (KCONV, INNER), KCONV ** -0.5, 3.0, ((1, 2),)),
        "conv_bc": centred(streams_of[5], (KCONV, 2 * NS), KCONV ** -0.5, 3.0),
        "a_log": draw_a_log(jax.random.fold_in(streams_of[17], 71), part),
        "dt_bias": jnp.clip(jax.random.uniform(streams_of[7], (HEADS,), jnp.float32, -1.0, 1.0) * level_of(streams_of[7], (HEADS,), ((0, 2),), -0.4, 0.0), -1.0, 1.0),
        "d_skip": draw_d_skip(jax.random.fold_in(streams_of[17], 71), part),
        "norm_gain": jnp.clip(1.0 + 0.15 * jax.random.normal(streams_of[9], (INNER,), jnp.float32), 0.25, 1.75),
        "out_weight": centred(streams_of[10], (D, INNER), INNER ** -0.5, 0.09375, ((0, 8), (1, 2))),
        "store_ssm": centred(part_keys[11], (STORE, HEADS, P_SIZE, NS), 1.0, 6.0, ((0, 8), (1, 2)), jnp.float32),
        "stored_conv_inputs": centred(part_keys[12], (STORE, KCONV - 1, INNER), 1.0, 6.0, ((0, 8), (2, 2)), jnp.float32),
        "store_convbc": centred(part_keys[13], (STORE, KCONV - 1, 2 * NS), 1.0, 6.0, ((0, 8),), jnp.float32),
        "hits": draw_hits(jax.random.fold_in(jax.random.fold_in(streams_of[17], part), 71), part),
        "assign": jax.random.permutation(part_keys[15], REQUESTS).astype(jnp.int32),
        "lengths": draw_lengths(jax.random.fold_in(jax.random.fold_in(streams_of[17], part), 71), part),
    }


def conv_silu(prev, current, weight):
    length = current.shape[0]
    seq = jnp.concatenate([prev, current.astype(jnp.float32)], axis=0)
    total = jnp.zeros(current.shape, jnp.float32)
    for k in range(weight.shape[0]):
        total = total + weight[k].astype(jnp.float32) * seq[k:k + length]
    return jax.nn.silu(total).astype(jnp.bfloat16)

def block_step(state, inputs):
    x_block, b_block, readout_tile, dt_block, rate_block = inputs
    cum = jnp.cumsum(rate_block, axis=0)
    scores = jnp.dot(readout_tile, b_block.T, preferred_element_type=jnp.float32)
    cum_heads = cum.T
    diff = cum_heads[:, :, None] - cum_heads[:, None, :]
    size = cum.shape[0]
    causal = jnp.arange(size)[:, None] >= jnp.arange(size)[None, :]
    decay = jnp.exp(jnp.where(causal[None], diff, -jnp.inf))
    parameter_tensors = (scores[None] * decay * dt_block.T[:, None, :]).astype(jnp.bfloat16)
    intra = jnp.einsum('hts,shp->thp', parameter_tensors.astype(jnp.float32), x_block.astype(jnp.float32))
    from_state = jnp.exp(cum)[:, :, None] * jnp.einsum('tn,hpn->thp', readout_tile.astype(jnp.float32), state, precision=lax.Precision.HIGHEST)
    ending = cum[-1]
    coef = jnp.exp(ending[None, :] - cum) * dt_block
    update = jnp.einsum('shp,sn->hpn', x_block.astype(jnp.float32) * coef[:, :, None], b_block.astype(jnp.float32), precision=lax.Precision.HIGHEST)
    new_state = jnp.exp(ending)[:, None, None] * state + update
    return (new_state, intra + from_state)

def reference(x_in, z_in, bc_in, dt_in, conv_x, conv_bc, a_log, dt_bias, d_skip, norm_gain, out_weight, store_ssm, stored_conv_inputs, store_convbc, hits, assign, lengths):
    owner = hits[:, 0]
    slot = hits[:, 1]
    rows = (owner[assign] * SLOTS + slot[assign]).astype(jnp.int32)
    decay_rate = -jnp.exp(a_log)
    nblocks = L // BLOCK

    def one(args):
        q_x, q_z, q_bc, q_dt, row, length = args
        xs = conv_silu(stored_conv_inputs[row], q_x, conv_x)
        bcs = conv_silu(store_convbc[row], q_bc, conv_bc)
        b_all = bcs[:, :NS]
        c_all = bcs[:, NS:]
        dt = jax.nn.softplus(q_dt + dt_bias[None, :])
        rate = dt * decay_rate[None, :]
        x3 = xs.reshape(L, HEADS, P_SIZE)
        inputs = (x3.reshape(nblocks, BLOCK, HEADS, P_SIZE), b_all.reshape(nblocks, BLOCK, NS), c_all.reshape(nblocks, BLOCK, NS), dt.reshape(nblocks, BLOCK, HEADS), rate.reshape(nblocks, BLOCK, HEADS))
        final, outs = lax.scan(block_step, store_ssm[row], inputs)
        ssm_out = outs.reshape(L, HEADS, P_SIZE) + d_skip[None, :, None] * x3.astype(jnp.float32)
        gated = ssm_out.reshape(L, INNER) * jax.nn.silu(q_z.astype(jnp.float32))
        mean_sq = lax.optimization_barrier(jnp.mean(gated * gated, axis=1))
        normed = (gated * lax.rsqrt(mean_sq + 1e-05)[:, None] * norm_gain[None, :]).astype(jnp.bfloat16)
        mixed = lax.dot_general(normed, out_weight, (((1,), (1,)), ((), ())), preferred_element_type=jnp.float32)
        valid = jnp.arange(L) < length
        return jnp.where(valid[:, None], mixed, 0.0).astype(jnp.bfloat16)
    outs = lax.map(one, (x_in.reshape(REQUESTS, L, INNER), z_in.reshape(REQUESTS, L, INNER), bc_in.reshape(REQUESTS, L, 2 * NS), dt_in.reshape(REQUESTS, L, HEADS), rows, lengths))
    return outs.reshape(TOKENS, D)
```

```python
import functools

import jax
import jax.numpy as jnp
from jax import lax
from jax.experimental import pallas as pl
from jax.experimental.pallas import tpu as pltpu
from jax.sharding import PartitionSpec as P

BLOCK = 128
INNER = 4096
LOG2E = 1.4426950408889634
GROUP = 8
NEG = -1e30


def silu(u):
    return u * (0.5 * jnp.tanh(0.5 * u) + 0.5)


def conv_silu(prev, current, weight):
    length = current.shape[0]
    seq = jnp.concatenate([prev, current.astype(jnp.float32)], axis=0)
    total = jnp.zeros(current.shape, jnp.float32)
    for k in range(weight.shape[0]):
        total = total + weight[k].astype(jnp.float32) * seq[k : k + length]
    return silu(total).astype(jnp.bfloat16)


def dot(a, b):
    return jnp.dot(a, b, preferred_element_type=jnp.float32)


def spread(cols, first, head, rows, lane, width):
    left = jnp.broadcast_to(cols[rows, first + head : first + head + 1], (BLOCK, 2 * width))
    right = jnp.broadcast_to(
        cols[rows, first + head + 1 : first + head + 2], (BLOCK, 2 * width)
    )
    return left, right, jnp.where(lane < width, left, right)


def scan_kernel(x_ref, prev_ref, taps_ref, cols_ref, arow_ref, skip_ref, g_ref, bt_ref, c_ref, y_ref, seq, xs):
    tokens, lanes = x_ref.shape
    nblocks = tokens // BLOCK
    width = lanes // GROUP
    pair = 2 * width
    taps = taps_ref.shape[0]
    seq[0:8, :] = prev_ref[...]
    for k in range(nblocks):
        seq[8 + k * BLOCK : 8 + (k + 1) * BLOCK, :] = x_ref[
            k * BLOCK : (k + 1) * BLOCK, :
        ].astype(jnp.float32)
    for k in range(nblocks):
        base = 8 - (taps - 1) + k * BLOCK
        total = taps_ref[0:1, :].astype(jnp.float32) * seq[base : base + BLOCK, :]
        for j in range(1, taps):
            total = total + taps_ref[j : j + 1, :].astype(jnp.float32) * seq[
                base + j : base + j + BLOCK, :
            ]
        xs[k * BLOCK : (k + 1) * BLOCK, :] = silu(total).astype(jnp.bfloat16)
    lane = lax.broadcasted_iota(jnp.int32, (BLOCK, pair), 1)
    causal = lax.broadcasted_iota(jnp.int32, (BLOCK, BLOCK), 0) >= lax.broadcasted_iota(
        jnp.int32, (BLOCK, BLOCK), 1
    )
    for p in range(GROUP // 2):
        here = slice(p * pair, (p + 1) * pair)
        head = 2 * p
        state = None
        for k in range(nblocks):
            rows = slice(k * BLOCK, (k + 1) * BLOCK)
            x2 = xs[rows, here]
            left, right, cum = spread(cols_ref, 0, head, rows, lane, width)
            weights = []
            for i, col in ((0, left), (1, right)):
                diff = col - arow_ref[head + i : head + i + 1, rows]
                decay = jnp.exp2(jnp.where(causal, diff, NEG))
                weights.append((decay * g_ref[rows, :]).astype(jnp.bfloat16))
            zero = jnp.zeros_like(x2)
            both = jnp.concatenate(
                [jnp.where(lane < width, x2, zero), jnp.where(lane < width, zero, x2)], axis=0
            )
            out = dot(jnp.concatenate(weights, axis=1), both)
            x2f = x2.astype(jnp.float32)
            out = out + skip_ref[:, here] * x2f
            if k > 0:
                out = out + jnp.exp2(cum) * dot(c_ref[rows, :], state.astype(jnp.bfloat16))
            y_ref[rows, here] = out
            if k < nblocks - 1:
                _, _, acol = spread(cols_ref, GROUP, head, rows, lane, width)
                end = cum[BLOCK - 1 : BLOCK, :]
                scaled = (x2f * jnp.exp2(end - acol)).astype(jnp.bfloat16)
                update = dot(bt_ref[:, rows], scaled)
                state = update if k == 0 else jnp.exp2(end) * state + update


def scan_call(x_in, prev, taps, cols, arow, skip, g, bt, c):
    tokens, channels = x_in.shape
    groups = cols.shape[0]
    lanes = channels // groups
    n = c.shape[1]
    return pl.pallas_call(
        scan_kernel,
        grid=(groups,),
        in_specs=[
            pl.BlockSpec((tokens, lanes), lambda i: (0, i)),
            pl.BlockSpec((8, lanes), lambda i: (0, i)),
            pl.BlockSpec((taps.shape[0], lanes), lambda i: (0, i)),
            pl.BlockSpec((None, tokens, 2 * GROUP), lambda i: (i, 0, 0)),
            pl.BlockSpec((GROUP, tokens), lambda i: (i, 0)),
            pl.BlockSpec((1, lanes), lambda i: (0, i)),
            pl.BlockSpec((tokens, BLOCK), lambda i: (0, 0)),
            pl.BlockSpec((n, tokens), lambda i: (0, 0)),
            pl.BlockSpec((tokens, n), lambda i: (0, 0)),
        ],
        out_specs=pl.BlockSpec((tokens, lanes), lambda i: (0, i)),
        out_shape=jax.ShapeDtypeStruct((tokens, channels), jnp.float32),
        scratch_shapes=[
            pltpu.VMEM((tokens + 8, lanes), jnp.float32),
            pltpu.VMEM((tokens, lanes), jnp.bfloat16),
        ],
        compiler_params=pltpu.CompilerParams(vmem_limit_bytes=40 * 2**20),
        cost_estimate=pl.CostEstimate(
            flops=2 * tokens * channels * 1024, bytes_accessed=tokens * channels * 6, transcendentals=tokens * channels * 4
        ),
        name="scan_blocks",
    )(x_in, prev, taps, cols, arow, skip, g, bt, c)


def gate_kernel(y_ref, z_ref, cols_ref, h_ref, c_ref, gain_ref, out_ref, sq_ref):
    tokens, lanes = y_ref.shape
    nblocks = tokens // BLOCK
    width = lanes // GROUP
    pair = 2 * width
    lane = lax.broadcasted_iota(jnp.int32, (BLOCK, pair), 1)

    @pl.when(pl.program_id(0) == 0)
    def _():
        sq_ref[...] = jnp.zeros_like(sq_ref)

    for k in range(nblocks):
        rows = slice(k * BLOCK, (k + 1) * BLOCK)
        read = lax.dot_general(
            c_ref[rows, :], h_ref[...], (((1,), (1,)), ((), ())), preferred_element_type=jnp.float32
        )
        total = sq_ref[rows, :]
        for p in range(GROUP // 2):
            here = slice(p * pair, (p + 1) * pair)
            _, _, cum = spread(cols_ref, 0, 2 * p, rows, lane, width)
            out = y_ref[rows, here] + jnp.exp2(cum) * read[:, here]
            gated = out * silu(z_ref[rows, here].astype(jnp.float32))
            total = total + gated * gated
            out_ref[rows, here] = (gated * gain_ref[:, here]).astype(jnp.bfloat16)
        sq_ref[rows, :] = total


def gate_call(y, z, cols, h, c, gain):
    tokens, channels = y.shape
    groups = cols.shape[0]
    lanes = channels // groups
    n = c.shape[1]
    return pl.pallas_call(
        gate_kernel,
        grid=(groups,),
        in_specs=[
            pl.BlockSpec((tokens, lanes), lambda i: (0, i)),
            pl.BlockSpec((tokens, lanes), lambda i: (0, i)),
            pl.BlockSpec((None, tokens, GROUP), lambda i: (i, 0, 0)),
            pl.BlockSpec((lanes, n), lambda i: (i, 0)),
            pl.BlockSpec((tokens, n), lambda i: (0, 0)),
            pl.BlockSpec((1, lanes), lambda i: (0, i)),
        ],
        out_specs=[
            pl.BlockSpec((tokens, lanes), lambda i: (0, i)),
            pl.BlockSpec((tokens, 128), lambda i: (0, 0)),
        ],
        out_shape=[
            jax.ShapeDtypeStruct((tokens, channels), jnp.bfloat16),
            jax.ShapeDtypeStruct((tokens, 128), jnp.float32),
        ],
        compiler_params=pltpu.CompilerParams(vmem_limit_bytes=40 * 2**20),
        cost_estimate=pl.CostEstimate(
            flops=2 * tokens * channels * 256, bytes_accessed=tokens * channels * 9, transcendentals=tokens * channels * 2
        ),
        name="gate_blocks",
    )(y, z, cols, h, c, gain)


def gather_all(value, axis):
    n = lax.axis_size(axis)
    if n & (n - 1):
        return lax.all_gather(value, axis, axis=0)
    me = lax.axis_index(axis)
    held = value[None]
    step = 1
    while step < n:
        other = lax.ppermute(held, axis, [(i, i ^ step) for i in range(n)])
        low = (me & step) == 0
        held = jnp.concatenate(
            [jnp.where(low, held, other), jnp.where(low, other, held)], axis=0
        )
        step *= 2
    return held


def ring_order(n):
    if n == 8:
        return [0, 2, 4, 6, 7, 5, 3, 1]
    return list(range(n))


def ring_gather(block, axis):
    n = lax.axis_size(axis)
    rows = block.shape[0]
    order = ring_order(n)
    place = [order.index(i) for i in range(n)]
    ahead = [(order[i], order[(i + 1) % n]) for i in range(n)]
    back = [(b, a) for a, b in ahead]
    me = jnp.asarray(place)[lax.axis_index(axis)]
    ids = jnp.asarray(order)
    full = jnp.zeros((n * rows, block.shape[1]), block.dtype)

    def put(full, piece, offset, first=0):
        at = ids[lax.rem(me + offset + n, n)] * rows + first
        return lax.dynamic_update_slice(full, piece, (at, 0))

    full = put(full, block, 0)
    a = b = block
    for k in range(1, (n - 1) // 2 + 1):
        a = lax.ppermute(a, axis, ahead)
        b = lax.ppermute(b, axis, back)
        full = put(put(full, a, -k), b, k)
    if n % 2 == 0:
        k = n // 2
        half = rows // 2
        full = put(full, lax.ppermute(a[:half], axis, ahead), -k)
        full = put(full, lax.ppermute(b[half:], axis, back), k, half)
    return full


def body(
    x_in,
    z_in,
    bc_in,
    dt_in,
    conv_x,
    conv_bc,
    a_log,
    dt_bias,
    d_skip,
    norm_gain,
    out_weight,
    store_ssm,
    stored_conv_inputs,
    store_convbc,
    hits,
    assign,
    lengths,
):
    ncache = lax.axis_size("cache")
    requests = hits.shape[0]
    local_slots, heads, width, n = store_ssm.shape
    taps_prev = stored_conv_inputs.shape[1]
    tokens, channels = x_in.shape
    nblocks = tokens // BLOCK
    groups = heads // GROUP

    row_of = hits[:, 0] * local_slots + hits[:, 1]
    position_hits = (assign[:, None] == jnp.arange(requests)[None, :]).astype(jnp.int32)
    row_at = jnp.sum(position_hits * row_of[None, :], axis=1)
    row_here = row_at[lax.axis_index("cache")]

    states = store_ssm.astype(jnp.bfloat16).reshape(local_slots, heads, width * n)
    states = lax.all_to_all(states, "cache", split_axis=1, concat_axis=0, tiled=True)
    states = jnp.take(states, row_at, axis=0)
    start = lax.all_to_all(states, "cache", split_axis=0, concat_axis=1, tiled=True)
    start = start.reshape(channels, n)

    small = jnp.concatenate([stored_conv_inputs, store_convbc], axis=2)
    small = gather_all(small.reshape(-1, 128), "cache")
    small = lax.dynamic_index_in_dim(
        small.reshape(ncache * local_slots, taps_prev, -1), row_here, 0, keepdims=False
    )
    prev_x = jnp.concatenate(
        [jnp.zeros((8 - taps_prev, channels), jnp.float32), small[:, :channels]], axis=0
    )

    weight = ring_gather(out_weight, "cache")

    bcs = conv_silu(small[:, channels:], bc_in, conv_bc)
    b = bcs[:, :n]
    c = bcs[:, n:]
    step_size = jax.nn.softplus(dt_in + dt_bias[None, :])
    rate = step_size * (-LOG2E * jnp.exp(a_log))[None, :]
    b3 = b.reshape(nblocks, BLOCK, n)
    c3 = c.reshape(nblocks, BLOCK, n)
    g = jnp.einsum("ktn,ksn->kts", c3, b3, preferred_element_type=jnp.float32)
    causal = jnp.arange(BLOCK)[:, None] >= jnp.arange(BLOCK)[None, :]
    g = jnp.where(causal[None], g, 0.0).reshape(tokens, BLOCK)
    cum = jnp.einsum(
        "ts,ksh->kth",
        causal.astype(jnp.float32),
        rate.reshape(nblocks, BLOCK, heads),
        precision=lax.Precision.HIGHEST,
    )
    ends = cum[:, -1, :]
    before = jnp.concatenate([jnp.zeros((1, heads), jnp.float32), jnp.cumsum(ends, axis=0)[:-1]])
    whole = (cum + before[:, None, :]).reshape(tokens, heads)
    cum = cum.reshape(tokens, heads)
    acol = cum - jnp.log2(step_size)

    def grouped(v):
        return v.reshape(tokens, groups, GROUP).transpose(1, 0, 2)

    cols = jnp.concatenate([grouped(cum), grouped(acol)], axis=2)
    skip = jnp.repeat(d_skip, width)[None, :]
    y = scan_call(x_in, prev_x, conv_x, cols, acol.T, skip, g, b.T, c)
    gated, squares = gate_call(y, z_in, grouped(whole), start, c, norm_gain[None, :])

    swap = [(0, 1), (1, 0)]
    half = weight.shape[0] // 2
    core = lax.axis_index("tensor")
    squares = jnp.sum(squares, axis=1)
    squares = squares + lax.ppermute(squares, "tensor", swap)

    def project(index):
        part = lax.dynamic_slice_in_dim(weight, index * half, half, 0)
        return lax.dot_general(
            gated, part, (((1,), (1,)), ((), ())), preferred_element_type=jnp.float32
        )

    other = lax.ppermute(project(1 - core).astype(jnp.bfloat16), "tensor", swap)
    summed = project(core) + other.astype(jnp.float32)
    mixed = summed * lax.rsqrt(squares / INNER + 1e-05)[:, None]
    valid = jnp.arange(tokens) < lengths[0]
    return jnp.where(valid[:, None], mixed, 0.0).astype(jnp.bfloat16)


def solution(mesh):
    return jax.shard_map(
        body,
        mesh=mesh,
        in_specs=(
            P(("groups", "cache"), "tensor"),
            P(("groups", "cache"), "tensor"),
            P(("groups", "cache"), None),
            P(("groups", "cache"), "tensor"),
            P(None, "tensor"),
            P(),
            P("tensor"),
            P("tensor"),
            P("tensor"),
            P("tensor"),
            P("cache", "tensor"),
            P(("groups", "cache"), "tensor", None, None),
            P(("groups", "cache"), None, "tensor"),
            P(("groups", "cache"), None, None),
            P("groups", None),
            P("groups"),
            P(("groups", "cache")),
        ),
        out_specs=P(("groups", "cache"), "tensor"),
        check_vma=False,
    )
```

```python
import functools

import jax
import jax.numpy as jnp
from jax import lax
from jax.experimental import pallas as pl
from jax.experimental.pallas import tpu as pltpu
from jax.sharding import PartitionSpec as P

BLOCK = 128
INNER = 4096
LOG2E = 1.4426950408889634
GROUP = 8
NEG = -1e30


def silu(u):
    return u * (0.5 * jnp.tanh(0.5 * u) + 0.5)


def conv_silu(prev, current, weight):
    length = current.shape[0]
    seq = jnp.concatenate([prev, current.astype(jnp.float32)], axis=0)
    total = jnp.zeros(current.shape, jnp.float32)
    for k in range(weight.shape[0]):
        total = total + weight[k].astype(jnp.float32) * seq[k : k + length]
    return silu(total).astype(jnp.bfloat16)


def dot(a, b):
    return jnp.dot(a, b, preferred_element_type=jnp.float32)


def spread(cols, first, head, rows, lane, width):
    left = jnp.broadcast_to(cols[rows, first + head : first + head + 1], (BLOCK, 2 * width))
    right = jnp.broadcast_to(
        cols[rows, first + head + 1 : first + head + 2], (BLOCK, 2 * width)
    )
    return left, right, jnp.where(lane < width, left, right)


def scan_kernel(x_ref, prev_ref, taps_ref, cols_ref, arow_ref, skip_ref, g_ref, bt_ref, c_ref, y_ref, seq, xs):
    tokens, lanes = x_ref.shape
    nblocks = tokens // BLOCK
    width = lanes // GROUP
    pair = 2 * width
    taps = taps_ref.shape[0]
    seq[0:8, :] = prev_ref[...]
    for k in range(nblocks):
        seq[8 + k * BLOCK : 8 + (k + 1) * BLOCK, :] = x_ref[
            k * BLOCK : (k + 1) * BLOCK, :
        ].astype(jnp.float32)
    for k in range(nblocks):
        base = 8 - (taps - 1) + k * BLOCK
        total = taps_ref[0:1, :].astype(jnp.float32) * seq[base : base + BLOCK, :]
        for j in range(1, taps):
            total = total + taps_ref[j : j + 1, :].astype(jnp.float32) * seq[
                base + j : base + j + BLOCK, :
            ]
        xs[k * BLOCK : (k + 1) * BLOCK, :] = silu(total).astype(jnp.bfloat16)
    lane = lax.broadcasted_iota(jnp.int32, (BLOCK, pair), 1)
    causal = lax.broadcasted_iota(jnp.int32, (BLOCK, BLOCK), 0) >= lax.broadcasted_iota(
        jnp.int32, (BLOCK, BLOCK), 1
    )
    for p in range(GROUP // 2):
        here = slice(p * pair, (p + 1) * pair)
        head = 2 * p
        state = None
        for k in range(nblocks):
            rows = slice(k * BLOCK, (k + 1) * BLOCK)
            x2 = xs[rows, here]
            left, right, cum = spread(cols_ref, 0, head, rows, lane, width)
            weights = []
            for i, col in ((0, left), (1, right)):
                diff = col - arow_ref[head + i : head + i + 1, rows]
                decay = jnp.exp2(jnp.where(causal, diff, NEG))
                weights.append((decay * g_ref[rows, :]).astype(jnp.bfloat16))
            zero = jnp.zeros_like(x2)
            both = jnp.concatenate(
                [jnp.where(lane < width, x2, zero), jnp.where(lane < width, zero, x2)], axis=0
            )
            out = dot(jnp.concatenate(weights, axis=1), both)
            x2f = x2.astype(jnp.float32)
            out = out + skip_ref[:, here] * x2f
            if k > 0:
                out = out + jnp.exp2(cum) * dot(c_ref[rows, :], state.astype(jnp.bfloat16))
            y_ref[rows, here] = out
            if k < nblocks - 1:
                _, _, acol = spread(cols_ref, GROUP, head, rows, lane, width)
                end = cum[BLOCK - 1 : BLOCK, :]
                scaled = (x2f * jnp.exp2(end - acol)).astype(jnp.bfloat16)
                update = dot(bt_ref[:, rows], scaled)
                state = update if k == 0 else jnp.exp2(end) * state + update


def scan_call(x_in, prev, taps, cols, arow, skip, g, bt, c):
    tokens, channels = x_in.shape
    groups = cols.shape[0]
    lanes = channels // groups
    n = c.shape[1]
    return pl.pallas_call(
        scan_kernel,
        grid=(groups,),
        in_specs=[
            pl.BlockSpec((tokens, lanes), lambda i: (0, i)),
            pl.BlockSpec((8, lanes), lambda i: (0, i)),
            pl.BlockSpec((taps.shape[0], lanes), lambda i: (0, i)),
            pl.BlockSpec((None, tokens, 2 * GROUP), lambda i: (i, 0, 0)),
            pl.BlockSpec((GROUP, tokens), lambda i: (i, 0)),
            pl.BlockSpec((1, lanes), lambda i: (0, i)),
            pl.BlockSpec((tokens, BLOCK), lambda i: (0, 0)),
            pl.BlockSpec((n, tokens), lambda i: (0, 0)),
            pl.BlockSpec((tokens, n), lambda i: (0, 0)),
        ],
        out_specs=pl.BlockSpec((tokens, lanes), lambda i: (0, i)),
        out_shape=jax.ShapeDtypeStruct((tokens, channels), jnp.float32),
        scratch_shapes=[
            pltpu.VMEM((tokens + 8, lanes), jnp.float32),
            pltpu.VMEM((tokens, lanes), jnp.bfloat16),
        ],
        compiler_params=pltpu.CompilerParams(vmem_limit_bytes=40 * 2**20),
        cost_estimate=pl.CostEstimate(
            flops=2 * tokens * channels * 1024, bytes_accessed=tokens * channels * 6, transcendentals=tokens * channels * 4
        ),
        name="scan_blocks",
    )(x_in, prev, taps, cols, arow, skip, g, bt, c)


def gate_kernel(y_ref, z_ref, cols_ref, h_ref, c_ref, gain_ref, out_ref, sq_ref):
    tokens, lanes = y_ref.shape
    nblocks = tokens // BLOCK
    width = lanes // GROUP
    pair = 2 * width
    lane = lax.broadcasted_iota(jnp.int32, (BLOCK, pair), 1)

    @pl.when(pl.program_id(0) == 0)
    def _():
        sq_ref[...] = jnp.zeros_like(sq_ref)

    for k in range(nblocks):
        rows = slice(k * BLOCK, (k + 1) * BLOCK)
        read = lax.dot_general(
            c_ref[rows, :], h_ref[...], (((1,), (1,)), ((), ())), preferred_element_type=jnp.float32
        )
        total = sq_ref[rows, :]
        for p in range(GROUP // 2):
            here = slice(p * pair, (p + 1) * pair)
            _, _, cum = spread(cols_ref, 0, 2 * p, rows, lane, width)
            out = y_ref[rows, here] + jnp.exp2(cum) * read[:, here]
            gated = out * silu(z_ref[rows, here].astype(jnp.float32))
            total = total + gated * gated
            out_ref[rows, here] = (gated * gain_ref[:, here]).astype(jnp.bfloat16)
        sq_ref[rows, :] = total


def gate_call(y, z, cols, h, c, gain, first):
    tokens, channels = y.shape
    lanes = channels // cols.shape[0]
    groups = h.shape[0] // lanes
    n = c.shape[1]
    return pl.pallas_call(
        gate_kernel,
        grid=(groups,),
        in_specs=[
            pl.BlockSpec((tokens, lanes), lambda i: (0, first + i)),
            pl.BlockSpec((tokens, lanes), lambda i: (0, first + i)),
            pl.BlockSpec((None, tokens, GROUP), lambda i: (first + i, 0, 0)),
            pl.BlockSpec((lanes, n), lambda i: (i, 0)),
            pl.BlockSpec((tokens, n), lambda i: (0, 0)),
            pl.BlockSpec((1, lanes), lambda i: (0, first + i)),
        ],
        out_specs=[
            pl.BlockSpec((tokens, lanes), lambda i: (0, i)),
            pl.BlockSpec((tokens, 128), lambda i: (0, 0)),
        ],
        out_shape=[
            jax.ShapeDtypeStruct((tokens, groups * lanes), jnp.bfloat16),
            jax.ShapeDtypeStruct((tokens, 128), jnp.float32),
        ],
        compiler_params=pltpu.CompilerParams(vmem_limit_bytes=40 * 2**20),
        cost_estimate=pl.CostEstimate(
            flops=2 * tokens * groups * lanes * 256,
            bytes_accessed=tokens * groups * lanes * 9,
            transcendentals=tokens * groups * lanes * 2,
        ),
        name="gate_blocks",
    )(y, z, cols, h, c, gain)


def assemble_kernel(count, rows_ref, *refs):
    pieces, out_ref, sems = refs[:count], refs[count], refs[count + 1]
    copies = []
    for i, piece in enumerate(pieces):
        at = pl.multiple_of(rows_ref[i], 16)
        copies.append(
            pltpu.make_async_copy(piece, out_ref.at[pl.ds(at, piece.shape[0]), :], sems.at[i])
        )
    for copy in copies:
        copy.start()
    for copy in copies:
        copy.wait()


def assemble(pieces, rows):
    total = sum(piece.shape[0] for piece in pieces)
    return pl.pallas_call(
        functools.partial(assemble_kernel, len(pieces)),
        in_specs=[pl.BlockSpec(memory_space=pltpu.SMEM)]
        + [pl.BlockSpec(memory_space=pl.ANY)] * len(pieces),
        out_specs=pl.BlockSpec(memory_space=pl.ANY),
        out_shape=jax.ShapeDtypeStruct((total, pieces[0].shape[1]), pieces[0].dtype),
        scratch_shapes=[pltpu.SemaphoreType.DMA((len(pieces),))],
        compiler_params=pltpu.CompilerParams(vmem_limit_bytes=16 * 2**20),
        cost_estimate=pl.CostEstimate(
            flops=0, bytes_accessed=2 * total * pieces[0].shape[1] * 2, transcendentals=0
        ),
        name="assemble_rows",
    )(jnp.stack(rows).astype(jnp.int32), *pieces)


def project_kernel(a_ref, b_ref, w_ref, send_ref, keep_ref):
    depth = a_ref.shape[1]
    part = lax.dot_general(
        a_ref[...], w_ref[:, :depth], (((1,), (1,)), ((), ())), preferred_element_type=jnp.float32
    ) + lax.dot_general(
        b_ref[...], w_ref[:, depth:], (((1,), (1,)), ((), ())), preferred_element_type=jnp.float32
    )

    @pl.when(pl.program_id(0) == 0)
    def _():
        send_ref[...] = part.astype(jnp.bfloat16)

    @pl.when(pl.program_id(0) == 1)
    def _():
        keep_ref[...] = part


def project(a, b, weight):
    tokens = a.shape[0]
    rows, channels = weight.shape
    half = rows // 2
    return pl.pallas_call(
        project_kernel,
        grid=(2,),
        in_specs=[
            pl.BlockSpec(a.shape, lambda i: (0, 0)),
            pl.BlockSpec(b.shape, lambda i: (0, 0)),
            pl.BlockSpec((half, channels), lambda i: (1 - i, 0)),
        ],
        out_specs=[
            pl.BlockSpec((tokens, half), lambda i: (0, 0)),
            pl.BlockSpec((tokens, half), lambda i: (0, 0)),
        ],
        out_shape=[
            jax.ShapeDtypeStruct((tokens, half), jnp.bfloat16),
            jax.ShapeDtypeStruct((tokens, half), jnp.float32),
        ],
        compiler_params=pltpu.CompilerParams(vmem_limit_bytes=40 * 2**20),
        cost_estimate=pl.CostEstimate(
            flops=2 * tokens * rows * channels,
            bytes_accessed=2 * (rows + tokens) * channels,
            transcendentals=0,
        ),
        name="project_rows",
    )(a, b, weight)


def combine_kernel(width, odd_ref, keep_ref, other_ref, back_ref, scale_ref, out_ref):
    mine = (keep_ref[...] + other_ref[...].astype(jnp.float32)) * scale_ref[...]
    back = back_ref[...].astype(jnp.float32) * scale_ref[...]
    even = odd_ref[0] == 0
    for i in range(mine.shape[1] // width):
        cols = slice(i * width, (i + 1) * width)
        first = jnp.where(even, mine[:, cols], back[:, cols])
        second = jnp.where(even, back[:, cols], mine[:, cols])
        out_ref[:, 2 * i * width : (2 * i + 2) * width] = jnp.concatenate(
            [first, second], axis=1
        ).astype(jnp.bfloat16)


def combine(odd, keep, other, back, scale, width):
    tokens, half = keep.shape
    return pl.pallas_call(
        functools.partial(combine_kernel, width),
        grid=(tokens // BLOCK,),
        in_specs=[pl.BlockSpec(memory_space=pltpu.SMEM)]
        + [pl.BlockSpec((BLOCK, half), lambda i: (i, 0))] * 3
        + [pl.BlockSpec((BLOCK, 1), lambda i: (i, 0))],
        out_specs=pl.BlockSpec((BLOCK, 2 * half), lambda i: (i, 0)),
        out_shape=jax.ShapeDtypeStruct((tokens, 2 * half), jnp.bfloat16),
        compiler_params=pltpu.CompilerParams(vmem_limit_bytes=16 * 2**20),
        name="combine_blocks",
    )(odd, keep, other, back, scale)


def gather_all(value, axis):
    n = lax.axis_size(axis)
    if n & (n - 1):
        return lax.all_gather(value, axis, axis=0)
    me = lax.axis_index(axis)
    held = value[None]
    step = 1
    while step < n:
        other = lax.ppermute(held, axis, [(i, i ^ step) for i in range(n)])
        low = (me & step) == 0
        held = jnp.concatenate(
            [jnp.where(low, held, other), jnp.where(low, other, held)], axis=0
        )
        step *= 2
    return held


def gather_parity(block, core):
    n = lax.axis_size("cache")
    me = lax.axis_index("cache")
    rows = block.shape[0]
    m = n // 2
    odd, spot = me % 2, me // 2

    def row(index, first=0):
        return lax.rem(index + m - core * (m // 2), m) * rows + first

    def swap(value, pairs):
        return lax.ppermute(
            value, "cache", [(2 * i + p, 2 * j + p) for i, j in pairs for p in (0, 1)]
        )

    if m == 4 and lax.axis_size("groups") == 2 and rows % 32 == 0:
        part = rows // 2
        side = lax.axis_index("groups")
        inner = (spot == 1) | (spot == 2)
        own = lax.dynamic_slice_in_dim(block, side * part, part, 0)

        def across(value):
            return lax.ppermute(value, "groups", [(0, 1), (1, 0)])

        pairs = [(0, 1), (1, 0), (2, 3), (3, 2)]
        middle = [(1, 2), (2, 1)]
        outward = [(1, 0), (2, 3)]
        mate, far = swap(own, pairs), swap(own, middle)
        mate, far = lax.optimization_barrier((mate, far))
        mate_other = across(mate)
        far_out, end = swap(far, outward), swap(mate, middle)
        far_out, end = lax.optimization_barrier((far_out, end))
        far = jnp.where(inner, far, far_out)
        far_other = across(far)
        end_out = swap(end, outward)
        end_out, mate_other = lax.optimization_barrier((end_out, mate_other))
        end = jnp.where(inner, end, end_out)
        end_other = across(end)
        at_far = jnp.where(spot < 2, 2, 1)
        at_end = jnp.where(spot < 2, 3, 0)
        here, there = side * part, (1 - side) * part
        pieces = [block, mate, mate_other, far, far_other, end, end_other]
        places = [
            row(spot),
            row(spot ^ 1, here),
            row(spot ^ 1, there),
            row(at_far, here),
            row(at_far, there),
            row(at_end, here),
            row(at_end, there),
        ]
        return pieces, places
    ahead = [(i, (i + 1) % m) for i in range(m)]
    back = [(j, i) for i, j in ahead]
    pieces, places = [block], [row(spot)]
    a = b = block
    for k in range(1, m // 2 + 1):
        a = swap(a, ahead)
        pieces.append(a)
        places.append(row(lax.rem(spot + m - k, m)))
        if 2 * k < m:
            b = swap(b, back)
            pieces.append(b)
            places.append(row(lax.rem(spot + k, m)))
    return pieces, places


def body(
    x_in,
    z_in,
    bc_in,
    dt_in,
    conv_x,
    conv_bc,
    a_log,
    dt_bias,
    d_skip,
    norm_gain,
    out_weight,
    store_ssm,
    stored_conv_inputs,
    store_convbc,
    hits,
    assign,
    lengths,
):
    ncache = lax.axis_size("cache")
    requests = hits.shape[0]
    local_slots, heads, width, n = store_ssm.shape
    taps_prev = stored_conv_inputs.shape[1]
    tokens, channels = x_in.shape
    nblocks = tokens // BLOCK
    groups = heads // GROUP

    row_of = hits[:, 0] * local_slots + hits[:, 1]
    position_hits = (assign[:, None] == jnp.arange(requests)[None, :]).astype(jnp.int32)
    row_at = jnp.sum(position_hits * row_of[None, :], axis=1)
    row_here = row_at[lax.axis_index("cache")]

    share = channels // (2 * ncache)
    states = store_ssm.astype(jnp.bfloat16).reshape(local_slots, 2, ncache, share, n)
    states = states.transpose(2, 0, 1, 3, 4)
    states = lax.all_to_all(states, "cache", split_axis=0, concat_axis=0, tiled=True)
    states = states.reshape(ncache * local_slots, 2, share, n)
    starts = []
    for part in range(2):
        chosen = jnp.take(states[:, part], row_at, axis=0)
        chosen = lax.all_to_all(chosen, "cache", split_axis=0, concat_axis=0, tiled=True)
        starts.append(chosen.reshape(channels // 2, n))

    small = jnp.concatenate([stored_conv_inputs, store_convbc], axis=2)
    small = gather_all(small.reshape(-1, 128), "cache")
    small = lax.dynamic_index_in_dim(
        small.reshape(ncache * local_slots, taps_prev, -1), row_here, 0, keepdims=False
    )
    prev_x = jnp.concatenate(
        [jnp.zeros((8 - taps_prev, channels), jnp.float32), small[:, :channels]], axis=0
    )

    core = lax.axis_index("tensor")
    pieces, places = gather_parity(out_weight, core)
    weight = assemble(pieces, places)

    bcs = conv_silu(small[:, channels:], bc_in, conv_bc)
    b = bcs[:, :n]
    c = bcs[:, n:]
    step_size = jax.nn.softplus(dt_in + dt_bias[None, :])
    rate = step_size * (-LOG2E * jnp.exp(a_log))[None, :]
    b3 = b.reshape(nblocks, BLOCK, n)
    c3 = c.reshape(nblocks, BLOCK, n)
    g = jnp.einsum("ktn,ksn->kts", c3, b3, preferred_element_type=jnp.float32)
    causal = jnp.arange(BLOCK)[:, None] >= jnp.arange(BLOCK)[None, :]
    g = jnp.where(causal[None], g, 0.0).reshape(tokens, BLOCK)
    cum = jnp.einsum(
        "ts,ksh->kth",
        causal.astype(jnp.float32),
        rate.reshape(nblocks, BLOCK, heads),
        precision=lax.Precision.HIGHEST,
    )
    ends = cum[:, -1, :]
    before = jnp.concatenate([jnp.zeros((1, heads), jnp.float32), jnp.cumsum(ends, axis=0)[:-1]])
    whole = (cum + before[:, None, :]).reshape(tokens, heads)
    cum = cum.reshape(tokens, heads)
    acol = cum - jnp.log2(step_size)

    def grouped(v):
        return v.reshape(tokens, groups, GROUP).transpose(1, 0, 2)

    cols = jnp.concatenate([grouped(cum), grouped(acol)], axis=2)
    skip = jnp.repeat(d_skip, width)[None, :]
    y = scan_call(x_in, prev_x, conv_x, cols, acol.T, skip, g, b.T, c)
    whole = grouped(whole)
    gain = norm_gain[None, :]
    cores = [(0, 1), (1, 0)]
    partners = [(i, i ^ 1) for i in range(ncache)]
    gated_a, squares_a = gate_call(y, z_in, whole, starts[0], c, gain, 0)
    theirs_a = lax.ppermute(gated_a, "cache", partners)
    gated_b, squares_b = gate_call(y, z_in, whole, starts[1], c, gain, groups // 2)
    theirs_b = lax.ppermute(gated_b, "cache", partners)
    squares = jnp.sum(squares_a + squares_b, axis=1)
    squares = squares + lax.ppermute(squares, "tensor", cores)
    valid = jnp.arange(tokens) < lengths[0]
    scale = jnp.where(valid, lax.rsqrt(squares / INNER + 1e-05), 0.0)[:, None]

    send, keep = project(gated_a, gated_b, weight)
    other = lax.ppermute(send, "tensor", cores)
    send, keep_back = project(theirs_a, theirs_b, weight)
    other_back = lax.ppermute(send, "tensor", cores)
    back = (keep_back + other_back.astype(jnp.float32)).astype(jnp.bfloat16)
    back = lax.ppermute(back, "cache", partners)
    odd = (lax.axis_index("cache") % 2).astype(jnp.int32)[None]
    return combine(odd, keep, other, back, scale, out_weight.shape[0])


def solution(mesh):
    return jax.shard_map(
        body,
        mesh=mesh,
        in_specs=(
            P(("groups", "cache"), "tensor"),
            P(("groups", "cache"), "tensor"),
            P(("groups", "cache"), None),
            P(("groups", "cache"), "tensor"),
            P(None, "tensor"),
            P(),
            P("tensor"),
            P("tensor"),
            P("tensor"),
            P("tensor"),
            P("cache", "tensor"),
            P(("groups", "cache"), "tensor", None, None),
            P(("groups", "cache"), None, "tensor"),
            P(("groups", "cache"), None, None),
            P("groups", None),
            P("groups"),
            P(("groups", "cache")),
        ),
        out_specs=P(("groups", "cache"), "tensor"),
        check_vma=False,
    )
```

```python
import functools

import jax
import jax.numpy as jnp
from jax import lax
from jax.experimental import pallas as pl
from jax.experimental.pallas import tpu as pltpu
from jax.sharding import PartitionSpec as P

BLOCK = 128
INNER = 4096
LOG2E = 1.4426950408889634
GROUP = 8
VMEM = 40 * 2**20
QUICK = pl.CostEstimate(flops=1, bytes_accessed=1, transcendentals=0)
NEG = -1e30


def silu(u):
    return u * (0.5 * jnp.tanh(0.5 * u) + 0.5)


def conv_silu(prev, current, weight):
    length = current.shape[0]
    seq = jnp.concatenate([prev, current.astype(jnp.float32)], axis=0)
    total = jnp.zeros(current.shape, jnp.float32)
    for k in range(weight.shape[0]):
        total = total + weight[k].astype(jnp.float32) * seq[k : k + length]
    return silu(total).astype(jnp.bfloat16)


def dot(a, b):
    return jnp.dot(a, b, preferred_element_type=jnp.float32)


def spread(cols, first, head, rows, lane, width):
    left = jnp.broadcast_to(cols[rows, first + head : first + head + 1], (BLOCK, 2 * width))
    right = jnp.broadcast_to(
        cols[rows, first + head + 1 : first + head + 2], (BLOCK, 2 * width)
    )
    return left, right, jnp.where(lane < width, left, right)


def scan_kernel(x_ref, prev_ref, taps_ref, cols_ref, arow_ref, skip_ref, g_ref, bt_ref, c_ref, y_ref, seq, xs):
    tokens, lanes = x_ref.shape
    nblocks = tokens // BLOCK
    width = lanes // GROUP
    pair = 2 * width
    taps = taps_ref.shape[0]
    seq[0:8, :] = prev_ref[...]
    for k in range(nblocks):
        seq[8 + k * BLOCK : 8 + (k + 1) * BLOCK, :] = x_ref[
            k * BLOCK : (k + 1) * BLOCK, :
        ].astype(jnp.float32)
    for k in range(nblocks):
        base = 8 - (taps - 1) + k * BLOCK
        total = taps_ref[0:1, :].astype(jnp.float32) * seq[base : base + BLOCK, :]
        for j in range(1, taps):
            total = total + taps_ref[j : j + 1, :].astype(jnp.float32) * seq[
                base + j : base + j + BLOCK, :
            ]
        xs[k * BLOCK : (k + 1) * BLOCK, :] = silu(total).astype(jnp.bfloat16)
    lane = lax.broadcasted_iota(jnp.int32, (BLOCK, pair), 1)
    causal = lax.broadcasted_iota(jnp.int32, (BLOCK, BLOCK), 0) >= lax.broadcasted_iota(
        jnp.int32, (BLOCK, BLOCK), 1
    )
    for p in range(GROUP // 2):
        here = slice(p * pair, (p + 1) * pair)
        head = 2 * p
        state = None
        for k in range(nblocks):
            rows = slice(k * BLOCK, (k + 1) * BLOCK)
            x2 = xs[rows, here]
            left, right, cum = spread(cols_ref, 0, head, rows, lane, width)
            weights = []
            for i, col in ((0, left), (1, right)):
                diff = col - arow_ref[head + i : head + i + 1, rows]
                decay = jnp.exp2(jnp.where(causal, diff, NEG))
                weights.append((decay * g_ref[rows, :]).astype(jnp.bfloat16))
            zero = jnp.zeros_like(x2)
            both = jnp.concatenate(
                [jnp.where(lane < width, x2, zero), jnp.where(lane < width, zero, x2)], axis=0
            )
            out = dot(jnp.concatenate(weights, axis=1), both)
            x2f = x2.astype(jnp.float32)
            out = out + skip_ref[:, here] * x2f
            if k > 0:
                out = out + jnp.exp2(cum) * dot(c_ref[rows, :], state.astype(jnp.bfloat16))
            y_ref[rows, here] = out
            if k < nblocks - 1:
                _, _, acol = spread(cols_ref, GROUP, head, rows, lane, width)
                end = cum[BLOCK - 1 : BLOCK, :]
                scaled = (x2f * jnp.exp2(end - acol)).astype(jnp.bfloat16)
                update = dot(bt_ref[:, rows], scaled)
                state = update if k == 0 else jnp.exp2(end) * state + update


def scan_call(x_in, prev, taps, cols, arow, skip, g, bt, c):
    tokens, channels = x_in.shape
    groups = cols.shape[0]
    lanes = channels // groups
    n = c.shape[1]
    return pl.pallas_call(
        scan_kernel,
        grid=(groups,),
        in_specs=[
            pl.BlockSpec((tokens, lanes), lambda i: (0, i)),
            pl.BlockSpec((8, lanes), lambda i: (0, i)),
            pl.BlockSpec((taps.shape[0], lanes), lambda i: (0, i)),
            pl.BlockSpec((None, tokens, 2 * GROUP), lambda i: (i, 0, 0)),
            pl.BlockSpec((GROUP, tokens), lambda i: (i, 0)),
            pl.BlockSpec((1, lanes), lambda i: (0, i)),
            pl.BlockSpec((tokens, BLOCK), lambda i: (0, 0)),
            pl.BlockSpec((n, tokens), lambda i: (0, 0)),
            pl.BlockSpec((tokens, n), lambda i: (0, 0)),
        ],
        out_specs=pl.BlockSpec((tokens, lanes), lambda i: (0, i)),
        out_shape=jax.ShapeDtypeStruct((tokens, channels), jnp.float32),
        scratch_shapes=[
            pltpu.VMEM((tokens + 8, lanes), jnp.float32),
            pltpu.VMEM((tokens, lanes), jnp.bfloat16),
        ],
        compiler_params=pltpu.CompilerParams(vmem_limit_bytes=VMEM),
        cost_estimate=QUICK,
        name="scan_blocks",
    )(x_in, prev, taps, cols, arow, skip, g, bt, c)


def gate_kernel(y_ref, z_ref, cols_ref, h_ref, c_ref, gain_ref, out_ref, sq_ref):
    tokens, lanes = y_ref.shape
    nblocks = tokens // BLOCK
    width = lanes // GROUP
    pair = 2 * width
    lane = lax.broadcasted_iota(jnp.int32, (BLOCK, pair), 1)

    @pl.when(pl.program_id(0) == 0)
    def _():
        sq_ref[...] = jnp.zeros_like(sq_ref)

    for k in range(nblocks):
        rows = slice(k * BLOCK, (k + 1) * BLOCK)
        read = lax.dot_general(
            c_ref[rows, :], h_ref[...], (((1,), (1,)), ((), ())), preferred_element_type=jnp.float32
        )
        total = sq_ref[rows, :]
        for p in range(GROUP // 2):
            here = slice(p * pair, (p + 1) * pair)
            _, _, cum = spread(cols_ref, 0, 2 * p, rows, lane, width)
            out = y_ref[rows, here] + jnp.exp2(cum) * read[:, here]
            gated = out * silu(z_ref[rows, here].astype(jnp.float32))
            total = total + gated * gated
            out_ref[rows, here] = (gated * gain_ref[:, here]).astype(jnp.bfloat16)
        sq_ref[rows, :] = total


def gate_call(y, z, cols, h, c, gain):
    tokens, channels = y.shape
    groups = cols.shape[0]
    lanes = channels // groups
    n = c.shape[1]
    return pl.pallas_call(
        gate_kernel,
        grid=(groups,),
        in_specs=[
            pl.BlockSpec((tokens, lanes), lambda i: (0, i)),
            pl.BlockSpec((tokens, lanes), lambda i: (0, i)),
            pl.BlockSpec((None, tokens, GROUP), lambda i: (i, 0, 0)),
            pl.BlockSpec((lanes, n), lambda i: (i, 0)),
            pl.BlockSpec((tokens, n), lambda i: (0, 0)),
            pl.BlockSpec((1, lanes), lambda i: (0, i)),
        ],
        out_specs=[
            pl.BlockSpec((tokens, lanes), lambda i: (0, i)),
            pl.BlockSpec((tokens, 128), lambda i: (0, 0)),
        ],
        out_shape=[
            jax.ShapeDtypeStruct((tokens, channels), jnp.bfloat16),
            jax.ShapeDtypeStruct((tokens, 128), jnp.float32),
        ],
        compiler_params=pltpu.CompilerParams(vmem_limit_bytes=VMEM),
        cost_estimate=QUICK,
        name="gate_blocks",
    )(y, z, cols, h, c, gain)


def project_kernel(cuts, rows_ref, mine_ref, value_ref, *refs):
    pieces, out_ref, held, sems = refs[:-3], refs[-3], refs[-2], refs[-1]
    copies = []
    for i, (piece, first, size) in enumerate(cuts):
        at = pl.multiple_of(rows_ref[i], 16)
        copies.append(
            pltpu.make_async_copy(
                pieces[piece].at[pl.ds(first, size), :],
                held.at[pl.ds(at, size), :],
                sems.at[i],
            )
        )
    for i, copy in enumerate(copies):
        pl.when(mine_ref[i] == 1)(copy.start)
    for i, copy in enumerate(copies):
        pl.when(mine_ref[i] == 1)(copy.wait)
    step = 256
    for first in range(0, out_ref.shape[1], step):
        cols = slice(first, min(first + step, out_ref.shape[1]))
        out_ref[:, cols] = lax.dot_general(
            value_ref[...], held[cols, :], (((1,), (1,)), ((), ())), preferred_element_type=jnp.float32
        ).astype(out_ref.dtype)


def project(value, pieces, cuts, rows, mine, total, dtype):
    tokens, channels = value.shape
    return pl.pallas_call(
        functools.partial(project_kernel, cuts),
        in_specs=[pl.BlockSpec(memory_space=pltpu.SMEM)] * 2
        + [pl.BlockSpec(memory_space=pltpu.VMEM)]
        + [pl.BlockSpec(memory_space=pl.ANY)] * len(pieces),
        out_specs=pl.BlockSpec(memory_space=pltpu.VMEM),
        out_shape=jax.ShapeDtypeStruct((tokens, total), dtype),
        scratch_shapes=[
            pltpu.VMEM((total, channels), pieces[0].dtype),
            pltpu.SemaphoreType.DMA((len(cuts),)),
        ],
        compiler_params=pltpu.CompilerParams(vmem_limit_bytes=60 * 2**20),
        cost_estimate=QUICK,
        name="project_rows",
    )(rows, mine, value, *pieces)


def choose_kernel(rows_ref, states_ref, out_ref, sems):
    copies = [
        pltpu.make_async_copy(states_ref.at[rows_ref[j]], out_ref.at[j], sems.at[j])
        for j in range(out_ref.shape[0])
    ]
    for copy in copies:
        copy.start()
    for copy in copies:
        copy.wait()


def choose(rows, states):
    count = rows.shape[0]
    return pl.pallas_call(
        choose_kernel,
        in_specs=[
            pl.BlockSpec(memory_space=pltpu.SMEM),
            pl.BlockSpec(memory_space=pl.ANY),
        ],
        out_specs=pl.BlockSpec(memory_space=pl.ANY),
        out_shape=jax.ShapeDtypeStruct((count, *states.shape[1:]), states.dtype),
        scratch_shapes=[pltpu.SemaphoreType.DMA((count,))],
        compiler_params=pltpu.CompilerParams(vmem_limit_bytes=16 * 2**20),
        cost_estimate=QUICK,
        name="choose_rows",
    )(rows, states)


def gather_all(value, axis):
    n = lax.axis_size(axis)
    if n & (n - 1):
        return lax.all_gather(value, axis, axis=0)
    me = lax.axis_index(axis)
    held = value[None]
    step = 1
    while step < n:
        other = lax.ppermute(held, axis, [(i, i ^ step) for i in range(n)])
        low = (me & step) == 0
        held = jnp.concatenate(
            [jnp.where(low, held, other), jnp.where(low, other, held)], axis=0
        )
        step *= 2
    return held


def gather_rows(block):
    n = lax.axis_size("cache")
    me = lax.axis_index("cache")
    rows = block.shape[0]
    spot = me // 2
    share = rows * 2 // 5
    if not (n == 8 and lax.axis_size("groups") == 2 and share % 16 == 0 and rows % 16 == 0):
        for _ in range(2):
            yield ()
        every = lax.all_gather(block, "cache", axis=0)
        yield [every[i] for i in range(n)], [(i, 0, rows, i, 0) for i in range(n)]
        return

    def swap(value, pairs):
        return lax.ppermute(
            value, "cache", [(2 * i + p, 2 * j + p) for i, j in pairs for p in (0, 1)]
        )

    def across(value):
        return lax.ppermute(value[:share], "groups", [(0, 1), (1, 0)])

    def beside(value):
        return lax.ppermute(value, "cache", [(i, i ^ 1) for i in range(n)])

    tie = lambda *values: lax.optimization_barrier(values)
    side = lax.axis_index("groups")
    inner = (spot == 1) | (spot == 2)
    own = jnp.concatenate(
        [lax.dynamic_slice_in_dim(block, side * share, share, 0), block[2 * share :]], axis=0
    )
    pairs = [(0, 1), (1, 0), (2, 3), (3, 2)]
    middle = [(1, 2), (2, 1)]
    outward = [(1, 0), (2, 3)]
    own_y, mate, far = beside(own), swap(own, pairs), swap(own, middle)
    own_y, mate, far = yield own_y, mate, far
    end, far_out, mate_y = swap(mate, middle), swap(far, outward), beside(mate)
    own_yx, mate_x = across(own_y), across(mate)
    end, far_out, mate_y, own_yx = tie(end, far_out, mate_y, own_yx)
    far = jnp.where(inner, far, far_out)
    end_out, far_y = swap(end, outward), beside(far)
    mate_yx, far_x = across(mate_y), across(far)
    end_out, far_y, mate_x, mate_yx, far_x = yield end_out, far_y, mate_x, mate_yx, far_x
    end = jnp.where(inner, end, end_out)
    end_y = beside(end)
    end_x, far_yx = across(end), across(far_y)
    end_yx = across(end_y)

    z_far, z_end = jnp.where(spot < 2, 2, 1), jnp.where(spot < 2, 3, 0)
    odd = me % 2
    pieces, cuts = [block], [(0, 0, rows, me, 0)]
    for index, plain, other in (
        (me ^ 1, own_y, own_yx),
        (me ^ 2, mate, mate_x),
        (me ^ 3, mate_y, mate_yx),
        (2 * z_far + odd, far, far_x),
        (2 * z_far + 1 - odd, far_y, far_yx),
        (2 * z_end + odd, end, end_x),
        (2 * z_end + 1 - odd, end_y, end_yx),
    ):
        at = len(pieces)
        pieces += [plain, other]
        cuts += [
            (at, 0, share, index, side * share),
            (at, share, rows - 2 * share, index, 2 * share),
            (at + 1, 0, share, index, (1 - side) * share),
        ]
    yield pieces, cuts


def body(
    x_in,
    z_in,
    bc_in,
    dt_in,
    conv_x,
    conv_bc,
    a_log,
    dt_bias,
    d_skip,
    norm_gain,
    out_weight,
    store_ssm,
    stored_conv_inputs,
    store_convbc,
    hits,
    assign,
    lengths,
):
    ncache = lax.axis_size("cache")
    requests = hits.shape[0]
    local_slots, heads, width, n = store_ssm.shape
    taps_prev = stored_conv_inputs.shape[1]
    tokens, channels = x_in.shape
    nblocks = tokens // BLOCK
    groups = heads // GROUP

    row_of = hits[:, 0] * local_slots + hits[:, 1]
    position_hits = (assign[:, None] == jnp.arange(requests)[None, :]).astype(jnp.int32)
    row_at = jnp.sum(position_hits * row_of[None, :], axis=1)
    row_here = row_at[lax.axis_index("cache")]

    def tie(*values):
        return lax.optimization_barrier(values)

    small = jnp.concatenate([stored_conv_inputs, store_convbc], axis=2)
    small = gather_all(small.reshape(-1, 128), "cache")
    gathered = gather_rows(out_weight)
    *step, store_ssm = tie(*next(gathered), store_ssm)
    step = gathered.send(tuple(step))

    share = channels // ncache
    states = store_ssm.astype(jnp.bfloat16).reshape(local_slots, ncache, share, n)
    states = states.transpose(1, 0, 2, 3)
    states, small = tie(states, small)
    states = lax.all_to_all(states, "cache", split_axis=0, concat_axis=0, tiled=True)
    chosen = choose(row_at.astype(jnp.int32), states.reshape(ncache * local_slots, share, n))

    small = lax.dynamic_index_in_dim(
        small.reshape(ncache * local_slots, taps_prev, -1), row_here, 0, keepdims=False
    )
    prev_x = jnp.concatenate(
        [jnp.zeros((8 - taps_prev, channels), jnp.float32), small[:, :channels]], axis=0
    )

    bcs = conv_silu(small[:, channels:], bc_in, conv_bc)
    b = bcs[:, :n]
    c = bcs[:, n:]
    step_size = jax.nn.softplus(dt_in + dt_bias[None, :])
    rate = step_size * (-LOG2E * jnp.exp(a_log))[None, :]
    b3 = b.reshape(nblocks, BLOCK, n)
    c3 = c.reshape(nblocks, BLOCK, n)
    g = jnp.einsum("ktn,ksn->kts", c3, b3, preferred_element_type=jnp.float32)
    causal = jnp.arange(BLOCK)[:, None] >= jnp.arange(BLOCK)[None, :]
    g = jnp.where(causal[None], g, 0.0).reshape(tokens, BLOCK)
    cum = jnp.einsum(
        "ts,ksh->kth",
        causal.astype(jnp.float32),
        rate.reshape(nblocks, BLOCK, heads),
        precision=lax.Precision.HIGHEST,
    )
    ends = cum[:, -1, :]
    before = jnp.concatenate([jnp.zeros((1, heads), jnp.float32), jnp.cumsum(ends, axis=0)[:-1]])
    whole = (cum + before[:, None, :]).reshape(tokens, heads)
    cum = cum.reshape(tokens, heads)
    acol = cum - jnp.log2(step_size)

    def grouped(v):
        return v.reshape(tokens, groups, GROUP).transpose(1, 0, 2)

    cols = jnp.concatenate([grouped(cum), grouped(acol)], axis=2)
    skip = jnp.repeat(d_skip, width)[None, :]
    y = scan_call(x_in, prev_x, conv_x, cols, acol.T, skip, g, b.T, c)
    whole = grouped(whole)
    gain = norm_gain[None, :]
    cores = [(0, 1), (1, 0)]
    core = lax.axis_index("tensor")
    start = lax.all_to_all(chosen, "cache", split_axis=0, concat_axis=0, tiled=True)
    start = start.reshape(channels, n)
    *step, y = tie(*step, y)
    pieces, cuts = gathered.send(tuple(step))
    gated, squares = gate_call(y, z_in, whole, start, c, gain)
    squares = jnp.sum(squares, axis=1)
    squares = squares + lax.ppermute(squares, "tensor", cores)
    valid = jnp.arange(tokens) < lengths[0]
    scale = jnp.where(valid, lax.rsqrt(squares / INNER + 1e-05), 0.0)[:, None]

    half = ncache // 2
    rows = out_weight.shape[0]
    places = jnp.stack(
        [lax.rem(jnp.int32(index), half) * rows + row for _, _, _, index, row in cuts]
    )
    owners = jnp.stack([jnp.int32(index) // half for _, _, _, index, _ in cuts])
    cuts = tuple(cut[:3] for cut in cuts)

    def products(owner, dtype):
        mine = (owners == owner).astype(jnp.int32)
        return project(gated, pieces, cuts, places.astype(jnp.int32), mine, half * rows, dtype)

    other = lax.ppermute(products(1 - core, jnp.bfloat16), "tensor", cores)
    summed = products(core, jnp.float32) + other.astype(jnp.float32)
    return (summed * scale).astype(jnp.bfloat16)


def solution(mesh):
    return jax.shard_map(
        body,
        mesh=mesh,
        in_specs=(
            P(("groups", "cache"), "tensor"),
            P(("groups", "cache"), "tensor"),
            P(("groups", "cache"), None),
            P(("groups", "cache"), "tensor"),
            P(None, "tensor"),
            P(),
            P("tensor"),
            P("tensor"),
            P("tensor"),
            P("tensor"),
            P("cache", "tensor"),
            P(("groups", "cache"), "tensor", None, None),
            P(("groups", "cache"), None, "tensor"),
            P(("groups", "cache"), None, None),
            P("groups", None),
            P("groups"),
            P(("groups", "cache")),
        ),
        out_specs=P(("groups", "cache"), "tensor"),
        check_vma=False,
    )
```

```python
import functools

import jax
import jax.numpy as jnp
from jax import lax
from jax.experimental import pallas as pl
from jax.experimental.pallas import tpu as pltpu
from jax.sharding import PartitionSpec as P

BLOCK = 128
INNER = 4096
LOG2E = 1.4426950408889634
GROUP = 8
VMEM = 40 * 2**20
QUICK = pl.CostEstimate(flops=1, bytes_accessed=1, transcendentals=0)
NEG = -1e30


def silu(u):
    return u * (0.5 * jnp.tanh(0.5 * u) + 0.5)


def conv_silu(prev, current, weight):
    length = current.shape[0]
    seq = jnp.concatenate([prev, current.astype(jnp.float32)], axis=0)
    total = jnp.zeros(current.shape, jnp.float32)
    for k in range(weight.shape[0]):
        total = total + weight[k].astype(jnp.float32) * seq[k : k + length]
    return silu(total).astype(jnp.bfloat16)


def dot(a, b):
    return jnp.dot(a, b, preferred_element_type=jnp.float32)


def spread(cols, first, head, rows, lane, width):
    left = jnp.broadcast_to(cols[rows, first + head : first + head + 1], (BLOCK, 2 * width))
    right = jnp.broadcast_to(
        cols[rows, first + head + 1 : first + head + 2], (BLOCK, 2 * width)
    )
    return left, right, jnp.where(lane < width, left, right)


def scan_kernel(x_ref, prev_ref, taps_ref, cols_ref, arow_ref, skip_ref, g_ref, bt_ref, c_ref, y_ref, seq, xs):
    tokens, lanes = x_ref.shape
    nblocks = tokens // BLOCK
    width = lanes // GROUP
    pair = 2 * width
    taps = taps_ref.shape[0]
    seq[0:8, :] = prev_ref[...]
    for k in range(nblocks):
        seq[8 + k * BLOCK : 8 + (k + 1) * BLOCK, :] = x_ref[
            k * BLOCK : (k + 1) * BLOCK, :
        ].astype(jnp.float32)
    for k in range(nblocks):
        base = 8 - (taps - 1) + k * BLOCK
        total = taps_ref[0:1, :].astype(jnp.float32) * seq[base : base + BLOCK, :]
        for j in range(1, taps):
            total = total + taps_ref[j : j + 1, :].astype(jnp.float32) * seq[
                base + j : base + j + BLOCK, :
            ]
        xs[k * BLOCK : (k + 1) * BLOCK, :] = silu(total).astype(jnp.bfloat16)
    lane = lax.broadcasted_iota(jnp.int32, (BLOCK, pair), 1)
    causal = lax.broadcasted_iota(jnp.int32, (BLOCK, BLOCK), 0) >= lax.broadcasted_iota(
        jnp.int32, (BLOCK, BLOCK), 1
    )
    for p in range(GROUP // 2):
        here = slice(p * pair, (p + 1) * pair)
        head = 2 * p
        state = None
        for k in range(nblocks):
            rows = slice(k * BLOCK, (k + 1) * BLOCK)
            x2 = xs[rows, here]
            left, right, cum = spread(cols_ref, 0, head, rows, lane, width)
            weights = []
            for i, col in ((0, left), (1, right)):
                diff = col - arow_ref[head + i : head + i + 1, rows]
                decay = jnp.exp2(jnp.where(causal, diff, NEG))
                weights.append((decay * g_ref[rows, :]).astype(jnp.bfloat16))
            zero = jnp.zeros_like(x2)
            both = jnp.concatenate(
                [jnp.where(lane < width, x2, zero), jnp.where(lane < width, zero, x2)], axis=0
            )
            out = dot(jnp.concatenate(weights, axis=1), both)
            x2f = x2.astype(jnp.float32)
            out = out + skip_ref[:, here] * x2f
            if k > 0:
                out = out + jnp.exp2(cum) * dot(c_ref[rows, :], state.astype(jnp.bfloat16))
            y_ref[rows, here] = out
            if k < nblocks - 1:
                _, _, acol = spread(cols_ref, GROUP, head, rows, lane, width)
                end = cum[BLOCK - 1 : BLOCK, :]
                scaled = (x2f * jnp.exp2(end - acol)).astype(jnp.bfloat16)
                update = dot(bt_ref[:, rows], scaled)
                state = update if k == 0 else jnp.exp2(end) * state + update


def scan_call(x_in, prev, taps, cols, arow, skip, g, bt, c):
    tokens, channels = x_in.shape
    groups = cols.shape[0]
    lanes = channels // groups
    n = c.shape[1]
    return pl.pallas_call(
        scan_kernel,
        grid=(groups,),
        in_specs=[
            pl.BlockSpec((tokens, lanes), lambda i: (0, i)),
            pl.BlockSpec((8, lanes), lambda i: (0, i)),
            pl.BlockSpec((taps.shape[0], lanes), lambda i: (0, i)),
            pl.BlockSpec((None, tokens, 2 * GROUP), lambda i: (i, 0, 0)),
            pl.BlockSpec((GROUP, tokens), lambda i: (i, 0)),
            pl.BlockSpec((1, lanes), lambda i: (0, i)),
            pl.BlockSpec((tokens, BLOCK), lambda i: (0, 0)),
            pl.BlockSpec((n, tokens), lambda i: (0, 0)),
            pl.BlockSpec((tokens, n), lambda i: (0, 0)),
        ],
        out_specs=pl.BlockSpec((tokens, lanes), lambda i: (0, i)),
        out_shape=jax.ShapeDtypeStruct((tokens, channels), jnp.float32),
        scratch_shapes=[
            pltpu.VMEM((tokens + 8, lanes), jnp.float32),
            pltpu.VMEM((tokens, lanes), jnp.bfloat16),
        ],
        compiler_params=pltpu.CompilerParams(vmem_limit_bytes=VMEM),
        cost_estimate=QUICK,
        name="scan_blocks",
    )(x_in, prev, taps, cols, arow, skip, g, bt, c)


def gate_kernel(y_ref, z_ref, cols_ref, h_ref, c_ref, gain_ref, out_ref, sq_ref):
    tokens, lanes = y_ref.shape
    nblocks = tokens // BLOCK
    width = lanes // GROUP
    pair = 2 * width
    lane = lax.broadcasted_iota(jnp.int32, (BLOCK, pair), 1)

    @pl.when(pl.program_id(0) == 0)
    def _():
        sq_ref[...] = jnp.zeros_like(sq_ref)

    for k in range(nblocks):
        rows = slice(k * BLOCK, (k + 1) * BLOCK)
        read = lax.dot_general(
            c_ref[rows, :], h_ref[...], (((1,), (1,)), ((), ())), preferred_element_type=jnp.float32
        )
        total = sq_ref[rows, :]
        for p in range(GROUP // 2):
            here = slice(p * pair, (p + 1) * pair)
            _, _, cum = spread(cols_ref, 0, 2 * p, rows, lane, width)
            out = y_ref[rows, here] + jnp.exp2(cum) * read[:, here]
            gated = out * silu(z_ref[rows, here].astype(jnp.float32))
            total = total + gated * gated
            out_ref[rows, here] = (gated * gain_ref[:, here]).astype(jnp.bfloat16)
        sq_ref[rows, :] = total


def gate_call(y, z, cols, h, c, gain):
    tokens, channels = y.shape
    groups = cols.shape[0]
    lanes = channels // groups
    n = c.shape[1]
    return pl.pallas_call(
        gate_kernel,
        grid=(groups,),
        in_specs=[
            pl.BlockSpec((tokens, lanes), lambda i: (0, i)),
            pl.BlockSpec((tokens, lanes), lambda i: (0, i)),
            pl.BlockSpec((None, tokens, GROUP), lambda i: (i, 0, 0)),
            pl.BlockSpec((lanes, n), lambda i: (i, 0)),
            pl.BlockSpec((tokens, n), lambda i: (0, 0)),
            pl.BlockSpec((1, lanes), lambda i: (0, i)),
        ],
        out_specs=[
            pl.BlockSpec((tokens, lanes), lambda i: (0, i)),
            pl.BlockSpec((tokens, 128), lambda i: (0, 0)),
        ],
        out_shape=[
            jax.ShapeDtypeStruct((tokens, channels), jnp.bfloat16),
            jax.ShapeDtypeStruct((tokens, 128), jnp.float32),
        ],
        compiler_params=pltpu.CompilerParams(vmem_limit_bytes=VMEM),
        cost_estimate=QUICK,
        name="gate_blocks",
    )(y, z, cols, h, c, gain)


def project_kernel(cuts, rows_ref, mine_ref, value_ref, *refs):
    pieces, out_ref, held, sems = refs[:-3], refs[-3], refs[-2], refs[-1]
    copies = []
    for i, (piece, first, size) in enumerate(cuts):
        at = pl.multiple_of(rows_ref[i], 16)
        copies.append(
            pltpu.make_async_copy(
                pieces[piece].at[pl.ds(first, size), :],
                held.at[pl.ds(at, size), :],
                sems.at[i],
            )
        )
    for i, copy in enumerate(copies):
        pl.when(mine_ref[i] == 1)(copy.start)
    for i, copy in enumerate(copies):
        pl.when(mine_ref[i] == 1)(copy.wait)
    step = 256
    for first in range(0, out_ref.shape[1], step):
        cols = slice(first, min(first + step, out_ref.shape[1]))
        out_ref[:, cols] = lax.dot_general(
            value_ref[...], held[cols, :], (((1,), (1,)), ((), ())), preferred_element_type=jnp.float32
        ).astype(out_ref.dtype)


def project(value, pieces, cuts, rows, mine, total, dtype):
    tokens, channels = value.shape
    return pl.pallas_call(
        functools.partial(project_kernel, cuts),
        in_specs=[pl.BlockSpec(memory_space=pltpu.SMEM)] * 2
        + [pl.BlockSpec(memory_space=pltpu.VMEM)]
        + [pl.BlockSpec(memory_space=pl.ANY)] * len(pieces),
        out_specs=pl.BlockSpec(memory_space=pltpu.VMEM),
        out_shape=jax.ShapeDtypeStruct((tokens, total), dtype),
        scratch_shapes=[
            pltpu.VMEM((total, channels), pieces[0].dtype),
            pltpu.SemaphoreType.DMA((len(cuts),)),
        ],
        compiler_params=pltpu.CompilerParams(vmem_limit_bytes=60 * 2**20),
        cost_estimate=QUICK,
        name="project_rows",
    )(rows, mine, value, *pieces)


def choose_kernel(rows_ref, states_ref, out_ref, sems):
    copies = [
        pltpu.make_async_copy(states_ref.at[rows_ref[j]], out_ref.at[j], sems.at[j])
        for j in range(out_ref.shape[0])
    ]
    for copy in copies:
        copy.start()
    for copy in copies:
        copy.wait()


def choose(rows, states):
    count = rows.shape[0]
    return pl.pallas_call(
        choose_kernel,
        in_specs=[
            pl.BlockSpec(memory_space=pltpu.SMEM),
            pl.BlockSpec(memory_space=pl.ANY),
        ],
        out_specs=pl.BlockSpec(memory_space=pl.ANY),
        out_shape=jax.ShapeDtypeStruct((count, *states.shape[1:]), states.dtype),
        scratch_shapes=[pltpu.SemaphoreType.DMA((count,))],
        compiler_params=pltpu.CompilerParams(vmem_limit_bytes=16 * 2**20),
        cost_estimate=QUICK,
        name="choose_rows",
    )(rows, states)


def gather_step(held, axis, step):
    n = lax.axis_size(axis)
    low = (lax.axis_index(axis) & step) == 0
    other = lax.ppermute(held, axis, [(i, i ^ step) for i in range(n)])
    return jnp.concatenate([jnp.where(low, held, other), jnp.where(low, other, held)], axis=0)


def gather_rows(block):
    n = lax.axis_size("cache")
    me = lax.axis_index("cache")
    rows = block.shape[0]
    spot = me // 2
    share = rows * 2 // 5
    if not (n == 8 and lax.axis_size("groups") == 2 and share % 16 == 0 and rows % 16 == 0):
        for _ in range(2):
            yield ()
        every = lax.all_gather(block, "cache", axis=0)
        yield [every[i] for i in range(n)], [(i, 0, rows, i, 0) for i in range(n)]
        return

    def swap(value, pairs):
        return lax.ppermute(
            value, "cache", [(2 * i + p, 2 * j + p) for i, j in pairs for p in (0, 1)]
        )

    def across(value):
        return lax.ppermute(value[:share], "groups", [(0, 1), (1, 0)])

    def beside(value):
        return lax.ppermute(value, "cache", [(i, i ^ 1) for i in range(n)])

    tie = lambda *values: lax.optimization_barrier(values)
    side = lax.axis_index("groups")
    inner = (spot == 1) | (spot == 2)
    own = jnp.concatenate(
        [lax.dynamic_slice_in_dim(block, side * share, share, 0), block[2 * share :]], axis=0
    )
    pairs = [(0, 1), (1, 0), (2, 3), (3, 2)]
    middle = [(1, 2), (2, 1)]
    outward = [(1, 0), (2, 3)]
    own_y, mate, far = beside(own), swap(own, pairs), swap(own, middle)
    own_y, mate, far = yield own_y, mate, far
    end, far_out, mate_y = swap(mate, middle), swap(far, outward), beside(mate)
    own_yx, mate_x = across(own_y), across(mate)
    end, far_out, mate_y, own_yx = tie(end, far_out, mate_y, own_yx)
    far = jnp.where(inner, far, far_out)
    end_out, far_y = swap(end, outward), beside(far)
    mate_yx, far_x = across(mate_y), across(far)
    end_out, far_y, mate_x, mate_yx, far_x = yield end_out, far_y, mate_x, mate_yx, far_x
    end = jnp.where(inner, end, end_out)
    end_y = beside(end)
    end_x = across(end)
    end_yx = beside(end_x)
    far_y, end_x = tie(far_y, end_x)
    far_yx = across(far_y)

    z_far, z_end = jnp.where(spot < 2, 2, 1), jnp.where(spot < 2, 3, 0)
    odd = me % 2
    pieces, cuts = [block], [(0, 0, rows, me, 0)]
    for index, plain, other in (
        (me ^ 1, own_y, own_yx),
        (me ^ 2, mate, mate_x),
        (me ^ 3, mate_y, mate_yx),
        (2 * z_far + odd, far, far_x),
        (2 * z_far + 1 - odd, far_y, far_yx),
        (2 * z_end + odd, end, end_x),
        (2 * z_end + 1 - odd, end_y, end_yx),
    ):
        at = len(pieces)
        pieces += [plain, other]
        cuts += [
            (at, 0, share, index, side * share),
            (at, share, rows - 2 * share, index, 2 * share),
            (at + 1, 0, share, index, (1 - side) * share),
        ]
    yield pieces, cuts


def body(
    x_in,
    z_in,
    bc_in,
    dt_in,
    conv_x,
    conv_bc,
    a_log,
    dt_bias,
    d_skip,
    norm_gain,
    out_weight,
    store_ssm,
    stored_conv_inputs,
    store_convbc,
    hits,
    assign,
    lengths,
):
    ncache = lax.axis_size("cache")
    requests = hits.shape[0]
    local_slots, heads, width, n = store_ssm.shape
    taps_prev = stored_conv_inputs.shape[1]
    tokens, channels = x_in.shape
    nblocks = tokens // BLOCK
    groups = heads // GROUP

    row_of = hits[:, 0] * local_slots + hits[:, 1]
    position_hits = (assign[:, None] == jnp.arange(requests)[None, :]).astype(jnp.int32)
    row_at = jnp.sum(position_hits * row_of[None, :], axis=1)
    row_here = row_at[lax.axis_index("cache")]

    def tie(*values):
        return lax.optimization_barrier(values)

    small = jnp.concatenate([stored_conv_inputs, store_convbc], axis=2)
    small = gather_step(small.reshape(1, -1, 128), "cache", 1)
    small, out_weight = tie(small, out_weight)
    size = 2
    while 2 * size < ncache:
        small = gather_step(small, "cache", size)
        size *= 2
    gathered = gather_rows(out_weight)
    *step, store_ssm, small = tie(*next(gathered), store_ssm, small)
    small = gather_step(small, "cache", size)
    step = gathered.send(tuple(step))

    share = channels // ncache
    states = store_ssm.astype(jnp.bfloat16).reshape(local_slots, ncache, share, n)
    states = states.transpose(1, 0, 2, 3)
    states, small = tie(states, small)
    states = lax.all_to_all(states, "cache", split_axis=0, concat_axis=0, tiled=True)
    chosen = choose(row_at.astype(jnp.int32), states.reshape(ncache * local_slots, share, n))

    small = lax.dynamic_index_in_dim(
        small.reshape(ncache * local_slots, taps_prev, -1), row_here, 0, keepdims=False
    )
    prev_x = jnp.concatenate(
        [jnp.zeros((8 - taps_prev, channels), jnp.float32), small[:, :channels]], axis=0
    )

    bcs = conv_silu(small[:, channels:], bc_in, conv_bc)
    b = bcs[:, :n]
    c = bcs[:, n:]
    step_size = jax.nn.softplus(dt_in + dt_bias[None, :])
    rate = step_size * (-LOG2E * jnp.exp(a_log))[None, :]
    b3 = b.reshape(nblocks, BLOCK, n)
    c3 = c.reshape(nblocks, BLOCK, n)
    g = jnp.einsum("ktn,ksn->kts", c3, b3, preferred_element_type=jnp.float32)
    causal = jnp.arange(BLOCK)[:, None] >= jnp.arange(BLOCK)[None, :]
    g = jnp.where(causal[None], g, 0.0).reshape(tokens, BLOCK)
    cum = jnp.einsum(
        "ts,ksh->kth",
        causal.astype(jnp.float32),
        rate.reshape(nblocks, BLOCK, heads),
        precision=lax.Precision.HIGHEST,
    )
    ends = cum[:, -1, :]
    before = jnp.concatenate([jnp.zeros((1, heads), jnp.float32), jnp.cumsum(ends, axis=0)[:-1]])
    whole = (cum + before[:, None, :]).reshape(tokens, heads)
    cum = cum.reshape(tokens, heads)
    acol = cum - jnp.log2(step_size)

    def grouped(v):
        return v.reshape(tokens, groups, GROUP).transpose(1, 0, 2)

    cols = jnp.concatenate([grouped(cum), grouped(acol)], axis=2)
    skip = jnp.repeat(d_skip, width)[None, :]
    y = scan_call(x_in, prev_x, conv_x, cols, acol.T, skip, g, b.T, c)
    whole = grouped(whole)
    gain = norm_gain[None, :]
    cores = [(0, 1), (1, 0)]
    core = lax.axis_index("tensor")
    start = lax.all_to_all(chosen, "cache", split_axis=0, concat_axis=0, tiled=True)
    start = start.reshape(channels, n)
    *step, y = tie(*step, y)
    pieces, cuts = gathered.send(tuple(step))
    gated, squares = gate_call(y, z_in, whole, start, c, gain)
    squares = jnp.sum(squares, axis=1)
    squares = squares + lax.ppermute(squares, "tensor", cores)
    valid = jnp.arange(tokens) < lengths[0]
    scale = jnp.where(valid, lax.rsqrt(squares / INNER + 1e-05), 0.0)[:, None]

    half = ncache // 2
    rows = out_weight.shape[0]
    places = jnp.stack(
        [lax.rem(jnp.int32(index), half) * rows + row for _, _, _, index, row in cuts]
    )
    owners = jnp.stack([jnp.int32(index) // half for _, _, _, index, _ in cuts])
    cuts = tuple(cut[:3] for cut in cuts)

    def products(owner, dtype):
        mine = (owners == owner).astype(jnp.int32)
        return project(gated, pieces, cuts, places.astype(jnp.int32), mine, half * rows, dtype)

    other = lax.ppermute(products(1 - core, jnp.bfloat16), "tensor", cores)
    summed = products(core, jnp.float32) + other.astype(jnp.float32)
    return (summed * scale).astype(jnp.bfloat16)


def solution(mesh):
    return jax.shard_map(
        body,
        mesh=mesh,
        in_specs=(
            P(("groups", "cache"), "tensor"),
            P(("groups", "cache"), "tensor"),
            P(("groups", "cache"), None),
            P(("groups", "cache"), "tensor"),
            P(None, "tensor"),
            P(),
            P("tensor"),
            P("tensor"),
            P("tensor"),
            P("tensor"),
            P("cache", "tensor"),
            P(("groups", "cache"), "tensor", None, None),
            P(("groups", "cache"), None, "tensor"),
            P(("groups", "cache"), None, None),
            P("groups", None),
            P("groups"),
            P(("groups", "cache")),
        ),
        out_specs=P(("groups", "cache"), "tensor"),
        check_vma=False,
    )
```

```python
import functools

import jax
import jax.numpy as jnp
from jax import lax
from jax.experimental import pallas as pl
from jax.experimental.pallas import tpu as pltpu
from jax.sharding import PartitionSpec as P

BLOCK = 128
INNER = 4096
LOG2E = 1.4426950408889634
GROUP = 8
VMEM = 40 * 2**20
QUICK = pl.CostEstimate(flops=1, bytes_accessed=1, transcendentals=0)
NEG = -1e30


def silu(u):
    return u * (0.5 * jnp.tanh(0.5 * u) + 0.5)


def conv_silu(prev, current, weight):
    length = current.shape[0]
    seq = jnp.concatenate([prev, current.astype(jnp.float32)], axis=0)
    total = jnp.zeros(current.shape, jnp.float32)
    for k in range(weight.shape[0]):
        total = total + weight[k].astype(jnp.float32) * seq[k : k + length]
    return silu(total).astype(jnp.bfloat16)


def dot(a, b):
    return jnp.dot(a, b, preferred_element_type=jnp.float32)


def spread(cols, first, head, rows, lane, width):
    left = jnp.broadcast_to(cols[rows, first + head : first + head + 1], (BLOCK, 2 * width))
    right = jnp.broadcast_to(
        cols[rows, first + head + 1 : first + head + 2], (BLOCK, 2 * width)
    )
    return left, right, jnp.where(lane < width, left, right)


def scan_kernel(x_ref, prev_ref, taps_ref, cols_ref, arow_ref, skip_ref, g_ref, bt_ref, c_ref, y_ref, seq, xs):
    tokens, lanes = x_ref.shape
    nblocks = tokens // BLOCK
    width = lanes // GROUP
    pair = 2 * width
    taps = taps_ref.shape[0]
    seq[0:8, :] = prev_ref[...]
    for k in range(nblocks):
        seq[8 + k * BLOCK : 8 + (k + 1) * BLOCK, :] = x_ref[
            k * BLOCK : (k + 1) * BLOCK, :
        ].astype(jnp.float32)
    for k in range(nblocks):
        base = 8 - (taps - 1) + k * BLOCK
        total = taps_ref[0:1, :].astype(jnp.float32) * seq[base : base + BLOCK, :]
        for j in range(1, taps):
            total = total + taps_ref[j : j + 1, :].astype(jnp.float32) * seq[
                base + j : base + j + BLOCK, :
            ]
        xs[k * BLOCK : (k + 1) * BLOCK, :] = silu(total).astype(jnp.bfloat16)
    lane = lax.broadcasted_iota(jnp.int32, (BLOCK, pair), 1)
    causal = lax.broadcasted_iota(jnp.int32, (BLOCK, BLOCK), 0) >= lax.broadcasted_iota(
        jnp.int32, (BLOCK, BLOCK), 1
    )
    for p in range(GROUP // 2):
        here = slice(p * pair, (p + 1) * pair)
        head = 2 * p
        state = None
        for k in range(nblocks):
            rows = slice(k * BLOCK, (k + 1) * BLOCK)
            x2 = xs[rows, here]
            left, right, cum = spread(cols_ref, 0, head, rows, lane, width)
            weights = []
            for i, col in ((0, left), (1, right)):
                diff = col - arow_ref[head + i : head + i + 1, rows]
                decay = jnp.exp2(jnp.where(causal, diff, NEG))
                weights.append((decay * g_ref[rows, :]).astype(jnp.bfloat16))
            zero = jnp.zeros_like(x2)
            both = jnp.concatenate(
                [jnp.where(lane < width, x2, zero), jnp.where(lane < width, zero, x2)], axis=0
            )
            out = dot(jnp.concatenate(weights, axis=1), both)
            x2f = x2.astype(jnp.float32)
            out = out + skip_ref[:, here] * x2f
            if k > 0:
                out = out + jnp.exp2(cum) * dot(c_ref[rows, :], state.astype(jnp.bfloat16))
            y_ref[rows, here] = out
            if k < nblocks - 1:
                _, _, acol = spread(cols_ref, GROUP, head, rows, lane, width)
                end = cum[BLOCK - 1 : BLOCK, :]
                scaled = (x2f * jnp.exp2(end - acol)).astype(jnp.bfloat16)
                update = dot(bt_ref[:, rows], scaled)
                state = update if k == 0 else jnp.exp2(end) * state + update


def scan_call(x_in, prev, taps, cols, arow, skip, g, bt, c):
    tokens, channels = x_in.shape
    groups = cols.shape[0]
    lanes = channels // groups
    n = c.shape[1]
    return pl.pallas_call(
        scan_kernel,
        grid=(groups,),
        in_specs=[
            pl.BlockSpec((tokens, lanes), lambda i: (0, i)),
            pl.BlockSpec((8, lanes), lambda i: (0, i)),
            pl.BlockSpec((taps.shape[0], lanes), lambda i: (0, i)),
            pl.BlockSpec((None, tokens, 2 * GROUP), lambda i: (i, 0, 0)),
            pl.BlockSpec((GROUP, tokens), lambda i: (i, 0)),
            pl.BlockSpec((1, lanes), lambda i: (0, i)),
            pl.BlockSpec((tokens, BLOCK), lambda i: (0, 0)),
            pl.BlockSpec((n, tokens), lambda i: (0, 0)),
            pl.BlockSpec((tokens, n), lambda i: (0, 0)),
        ],
        out_specs=pl.BlockSpec((tokens, lanes), lambda i: (0, i)),
        out_shape=jax.ShapeDtypeStruct((tokens, channels), jnp.float32),
        scratch_shapes=[
            pltpu.VMEM((tokens + 8, lanes), jnp.float32),
            pltpu.VMEM((tokens, lanes), jnp.bfloat16),
        ],
        compiler_params=pltpu.CompilerParams(vmem_limit_bytes=VMEM),
        cost_estimate=QUICK,
        name="scan_blocks",
    )(x_in, prev, taps, cols, arow, skip, g, bt, c)


def gate_kernel(y_ref, z_ref, cols_ref, h_ref, c_ref, gain_ref, out_ref, sq_ref):
    tokens, lanes = y_ref.shape
    nblocks = tokens // BLOCK
    width = lanes // GROUP
    pair = 2 * width
    lane = lax.broadcasted_iota(jnp.int32, (BLOCK, pair), 1)

    @pl.when(pl.program_id(0) == 0)
    def _():
        sq_ref[...] = jnp.zeros_like(sq_ref)

    for k in range(nblocks):
        rows = slice(k * BLOCK, (k + 1) * BLOCK)
        read = lax.dot_general(
            c_ref[rows, :], h_ref[...], (((1,), (1,)), ((), ())), preferred_element_type=jnp.float32
        )
        total = sq_ref[rows, :]
        for p in range(GROUP // 2):
            here = slice(p * pair, (p + 1) * pair)
            _, _, cum = spread(cols_ref, 0, 2 * p, rows, lane, width)
            out = y_ref[rows, here] + jnp.exp2(cum) * read[:, here]
            gated = out * silu(z_ref[rows, here].astype(jnp.float32))
            total = total + gated * gated
            out_ref[rows, here] = (gated * gain_ref[:, here]).astype(jnp.bfloat16)
        sq_ref[rows, :] = total


def gate_call(y, z, cols, h, c, gain):
    tokens, channels = y.shape
    groups = cols.shape[0]
    lanes = channels // groups
    n = c.shape[1]
    return pl.pallas_call(
        gate_kernel,
        grid=(groups,),
        in_specs=[
            pl.BlockSpec((tokens, lanes), lambda i: (0, i)),
            pl.BlockSpec((tokens, lanes), lambda i: (0, i)),
            pl.BlockSpec((None, tokens, GROUP), lambda i: (i, 0, 0)),
            pl.BlockSpec((lanes, n), lambda i: (i, 0)),
            pl.BlockSpec((tokens, n), lambda i: (0, 0)),
            pl.BlockSpec((1, lanes), lambda i: (0, i)),
        ],
        out_specs=[
            pl.BlockSpec((tokens, lanes), lambda i: (0, i)),
            pl.BlockSpec((tokens, 128), lambda i: (0, 0)),
        ],
        out_shape=[
            jax.ShapeDtypeStruct((tokens, channels), jnp.bfloat16),
            jax.ShapeDtypeStruct((tokens, 128), jnp.float32),
        ],
        compiler_params=pltpu.CompilerParams(vmem_limit_bytes=VMEM),
        cost_estimate=QUICK,
        name="gate_blocks",
    )(y, z, cols, h, c, gain)


def project_kernel(cuts, rows_ref, mine_ref, value_ref, *refs):
    pieces, out_ref, value, held, total, sems = refs[:-5], *refs[-5:]
    depth = value.shape[1] // 2
    loads = []
    for half in range(2):
        span = slice(half * depth, (half + 1) * depth)
        whole = pltpu.make_async_copy(
            value_ref.at[:, span], value.at[:, span], sems.at[half, len(cuts)]
        )
        whole.start()
        copies = []
        for i, (piece, first, size) in enumerate(cuts):
            at = pl.multiple_of(rows_ref[i], 16)
            copy = pltpu.make_async_copy(
                pieces[piece].at[pl.ds(first, size), span],
                held.at[pl.ds(at, size), span],
                sems.at[half, i],
            )
            pl.when(mine_ref[i] == 1)(copy.start)
            copies.append(copy)
        loads.append((span, whole, copies))
    step = 256
    for half, (span, whole, copies) in enumerate(loads):
        whole.wait()
        for i, copy in enumerate(copies):
            pl.when(mine_ref[i] == 1)(copy.wait)
        for at in range(0, out_ref.shape[1], step):
            cols = slice(at, min(at + step, out_ref.shape[1]))
            part = lax.dot_general(
                value[:, span],
                held[cols, span],
                (((1,), (1,)), ((), ())),
                preferred_element_type=jnp.float32,
            )
            if half == 0:
                total[:, cols] = part
            else:
                out_ref[:, cols] = (total[:, cols] + part).astype(out_ref.dtype)


def project(value, pieces, cuts, rows, mine, total, dtype):
    tokens, channels = value.shape
    return pl.pallas_call(
        functools.partial(project_kernel, cuts),
        in_specs=[pl.BlockSpec(memory_space=pltpu.SMEM)] * 2
        + [pl.BlockSpec(memory_space=pl.ANY)] * (1 + len(pieces)),
        out_specs=pl.BlockSpec(memory_space=pltpu.VMEM),
        out_shape=jax.ShapeDtypeStruct((tokens, total), dtype),
        scratch_shapes=[
            pltpu.VMEM((tokens, channels), value.dtype),
            pltpu.VMEM((total, channels), pieces[0].dtype),
            pltpu.VMEM((tokens, total), jnp.float32),
            pltpu.SemaphoreType.DMA((2, len(cuts) + 1)),
        ],
        compiler_params=pltpu.CompilerParams(vmem_limit_bytes=60 * 2**20),
        cost_estimate=QUICK,
        name="project_rows",
    )(rows, mine, value, *pieces)


def choose_kernel(rows_ref, states_ref, out_ref, sems):
    copies = [
        pltpu.make_async_copy(states_ref.at[rows_ref[j]], out_ref.at[j], sems.at[j])
        for j in range(out_ref.shape[0])
    ]
    for copy in copies:
        copy.start()
    for copy in copies:
        copy.wait()


def choose(rows, states):
    count = rows.shape[0]
    return pl.pallas_call(
        choose_kernel,
        in_specs=[
            pl.BlockSpec(memory_space=pltpu.SMEM),
            pl.BlockSpec(memory_space=pl.ANY),
        ],
        out_specs=pl.BlockSpec(memory_space=pl.ANY),
        out_shape=jax.ShapeDtypeStruct((count, *states.shape[1:]), states.dtype),
        scratch_shapes=[pltpu.SemaphoreType.DMA((count,))],
        compiler_params=pltpu.CompilerParams(vmem_limit_bytes=16 * 2**20),
        cost_estimate=QUICK,
        name="choose_rows",
    )(rows, states)


def gather_step(held, axis, step):
    n = lax.axis_size(axis)
    low = (lax.axis_index(axis) & step) == 0
    other = lax.ppermute(held, axis, [(i, i ^ step) for i in range(n)])
    return jnp.concatenate([jnp.where(low, held, other), jnp.where(low, other, held)], axis=0)


def gather_rows(block):
    n = lax.axis_size("cache")
    me = lax.axis_index("cache")
    rows = block.shape[0]
    spot = me // 2
    share = rows * 2 // 5
    if not (n == 8 and lax.axis_size("groups") == 2 and share % 16 == 0 and rows % 16 == 0):
        for _ in range(2):
            yield ()
        every = lax.all_gather(block, "cache", axis=0)
        yield [every[i] for i in range(n)], [(i, 0, rows, i, 0) for i in range(n)]
        return

    def swap(value, pairs):
        return lax.ppermute(
            value, "cache", [(2 * i + p, 2 * j + p) for i, j in pairs for p in (0, 1)]
        )

    def across(value):
        return lax.ppermute(value[:share], "groups", [(0, 1), (1, 0)])

    def beside(value):
        return lax.ppermute(value, "cache", [(i, i ^ 1) for i in range(n)])

    tie = lambda *values: lax.optimization_barrier(values)
    side = lax.axis_index("groups")
    inner = (spot == 1) | (spot == 2)
    own = jnp.concatenate(
        [lax.dynamic_slice_in_dim(block, side * share, share, 0), block[2 * share :]], axis=0
    )
    pairs = [(0, 1), (1, 0), (2, 3), (3, 2)]
    middle = [(1, 2), (2, 1)]
    outward = [(1, 0), (2, 3)]
    own_y, mate, far = beside(own), swap(own, pairs), swap(own, middle)
    own_y, mate, far = yield own_y, mate, far
    end, far_out, mate_y = swap(mate, middle), swap(far, outward), beside(mate)
    own_yx, mate_x = across(own_y), across(mate)
    end, far_out, mate_y, own_yx = tie(end, far_out, mate_y, own_yx)
    far = jnp.where(inner, far, far_out)
    end_out, far_y = swap(end, outward), beside(far)
    mate_yx, far_x = across(mate_y), across(far)
    end_out, far_y, mate_x, mate_yx, far_x = yield end_out, far_y, mate_x, mate_yx, far_x
    end = jnp.where(inner, end, end_out)
    end_y = beside(end)
    end_x = across(end)
    end_yx = beside(end_x)
    far_y, end_x = tie(far_y, end_x)
    far_yx = across(far_y)

    z_far, z_end = jnp.where(spot < 2, 2, 1), jnp.where(spot < 2, 3, 0)
    odd = me % 2
    pieces, cuts = [block], [(0, 0, rows, me, 0)]
    for index, plain, other in (
        (me ^ 1, own_y, own_yx),
        (me ^ 2, mate, mate_x),
        (me ^ 3, mate_y, mate_yx),
        (2 * z_far + odd, far, far_x),
        (2 * z_far + 1 - odd, far_y, far_yx),
        (2 * z_end + odd, end, end_x),
        (2 * z_end + 1 - odd, end_y, end_yx),
    ):
        at = len(pieces)
        pieces += [plain, other]
        cuts += [
            (at, 0, share, index, side * share),
            (at, share, rows - 2 * share, index, 2 * share),
            (at + 1, 0, share, index, (1 - side) * share),
        ]
    yield pieces, cuts


def body(
    x_in,
    z_in,
    bc_in,
    dt_in,
    conv_x,
    conv_bc,
    a_log,
    dt_bias,
    d_skip,
    norm_gain,
    out_weight,
    store_ssm,
    stored_conv_inputs,
    store_convbc,
    hits,
    assign,
    lengths,
):
    ncache = lax.axis_size("cache")
    requests = hits.shape[0]
    local_slots, heads, width, n = store_ssm.shape
    taps_prev = stored_conv_inputs.shape[1]
    tokens, channels = x_in.shape
    nblocks = tokens // BLOCK
    groups = heads // GROUP

    row_of = hits[:, 0] * local_slots + hits[:, 1]
    position_hits = (assign[:, None] == jnp.arange(requests)[None, :]).astype(jnp.int32)
    row_at = jnp.sum(position_hits * row_of[None, :], axis=1)
    row_here = row_at[lax.axis_index("cache")]

    def tie(*values):
        return lax.optimization_barrier(values)

    small = jnp.concatenate([stored_conv_inputs, store_convbc], axis=2)
    small = gather_step(small.reshape(1, -1, 128), "cache", 1)
    small, out_weight = tie(small, out_weight)
    size = 2
    while 2 * size < ncache:
        small = gather_step(small, "cache", size)
        size *= 2
    gathered = gather_rows(out_weight)
    *step, store_ssm, small = tie(*next(gathered), store_ssm, small)
    small = gather_step(small, "cache", size)
    step = gathered.send(tuple(step))

    share = channels // ncache
    states = store_ssm.astype(jnp.bfloat16).reshape(local_slots, ncache, share, n)
    states = states.transpose(1, 0, 2, 3)
    states, small = tie(states, small)
    states = lax.all_to_all(states, "cache", split_axis=0, concat_axis=0, tiled=True)
    chosen = choose(row_at.astype(jnp.int32), states.reshape(ncache * local_slots, share, n))

    small = lax.dynamic_index_in_dim(
        small.reshape(ncache * local_slots, taps_prev, -1), row_here, 0, keepdims=False
    )
    prev_x = jnp.concatenate(
        [jnp.zeros((8 - taps_prev, channels), jnp.float32), small[:, :channels]], axis=0
    )

    bcs = conv_silu(small[:, channels:], bc_in, conv_bc)
    b = bcs[:, :n]
    c = bcs[:, n:]
    step_size = jax.nn.softplus(dt_in + dt_bias[None, :])
    rate = step_size * (-LOG2E * jnp.exp(a_log))[None, :]
    b3 = b.reshape(nblocks, BLOCK, n)
    c3 = c.reshape(nblocks, BLOCK, n)
    g = jnp.einsum("ktn,ksn->kts", c3, b3, preferred_element_type=jnp.float32)
    causal = jnp.arange(BLOCK)[:, None] >= jnp.arange(BLOCK)[None, :]
    g = jnp.where(causal[None], g, 0.0).reshape(tokens, BLOCK)
    cum = jnp.einsum(
        "ts,ksh->kth",
        causal.astype(jnp.float32),
        rate.reshape(nblocks, BLOCK, heads),
        precision=lax.Precision.HIGHEST,
    )
    ends = cum[:, -1, :]
    before = jnp.concatenate([jnp.zeros((1, heads), jnp.float32), jnp.cumsum(ends, axis=0)[:-1]])
    whole = (cum + before[:, None, :]).reshape(tokens, heads)
    cum = cum.reshape(tokens, heads)
    acol = cum - jnp.log2(step_size)

    def grouped(v):
        return v.reshape(tokens, groups, GROUP).transpose(1, 0, 2)

    cols = jnp.concatenate([grouped(cum), grouped(acol)], axis=2)
    skip = jnp.repeat(d_skip, width)[None, :]
    y = scan_call(x_in, prev_x, conv_x, cols, acol.T, skip, g, b.T, c)
    whole = grouped(whole)
    gain = norm_gain[None, :]
    cores = [(0, 1), (1, 0)]
    core = lax.axis_index("tensor")
    start = lax.all_to_all(chosen, "cache", split_axis=0, concat_axis=0, tiled=True)
    start = start.reshape(channels, n)
    *step, y = tie(*step, y)
    pieces, cuts = gathered.send(tuple(step))
    gated, squares = gate_call(y, z_in, whole, start, c, gain)
    squares = jnp.sum(squares, axis=1)
    squares = squares + lax.ppermute(squares, "tensor", cores)
    valid = jnp.arange(tokens) < lengths[0]
    scale = jnp.where(valid, lax.rsqrt(squares / INNER + 1e-05), 0.0)[:, None]

    half = ncache // 2
    rows = out_weight.shape[0]
    places = jnp.stack(
        [lax.rem(jnp.int32(index), half) * rows + row for _, _, _, index, row in cuts]
    )
    owners = jnp.stack([jnp.int32(index) // half for _, _, _, index, _ in cuts])
    cuts = tuple(cut[:3] for cut in cuts)

    def products(owner, dtype):
        mine = (owners == owner).astype(jnp.int32)
        return project(gated, pieces, cuts, places.astype(jnp.int32), mine, half * rows, dtype)

    other = lax.ppermute(products(1 - core, jnp.bfloat16), "tensor", cores)
    summed = products(core, jnp.float32) + other.astype(jnp.float32)
    return (summed * scale).astype(jnp.bfloat16)


def solution(mesh):
    return jax.shard_map(
        body,
        mesh=mesh,
        in_specs=(
            P(("groups", "cache"), "tensor"),
            P(("groups", "cache"), "tensor"),
            P(("groups", "cache"), None),
            P(("groups", "cache"), "tensor"),
            P(None, "tensor"),
            P(),
            P("tensor"),
            P("tensor"),
            P("tensor"),
            P("tensor"),
            P("cache", "tensor"),
            P(("groups", "cache"), "tensor", None, None),
            P(("groups", "cache"), None, "tensor"),
            P(("groups", "cache"), None, None),
            P("groups", None),
            P("groups"),
            P(("groups", "cache")),
        ),
        out_specs=P(("groups", "cache"), "tensor"),
        check_vma=False,
    )
```

```python
import functools

import jax
import jax.numpy as jnp
from jax import lax
from jax.experimental import pallas as pl
from jax.experimental.pallas import tpu as pltpu
from jax.sharding import PartitionSpec as P

BLOCK = 128
INNER = 4096
LOG2E = 1.4426950408889634
GROUP = 8
VMEM = 40 * 2**20
QUICK = pl.CostEstimate(flops=1, bytes_accessed=1, transcendentals=0)
NEG = -1e30


def silu(u):
    return u * (0.5 * jnp.tanh(0.5 * u) + 0.5)


def conv_silu(prev, current, weight):
    length = current.shape[0]
    seq = jnp.concatenate([prev, current.astype(jnp.float32)], axis=0)
    total = jnp.zeros(current.shape, jnp.float32)
    for k in range(weight.shape[0]):
        total = total + weight[k].astype(jnp.float32) * seq[k : k + length]
    return silu(total).astype(jnp.bfloat16)


def dot(a, b):
    return jnp.dot(a, b, preferred_element_type=jnp.float32)


def spread(cols, first, head, rows, lane, width):
    left = jnp.broadcast_to(cols[rows, first + head : first + head + 1], (BLOCK, 2 * width))
    right = jnp.broadcast_to(
        cols[rows, first + head + 1 : first + head + 2], (BLOCK, 2 * width)
    )
    return left, right, jnp.where(lane < width, left, right)


def scan_kernel(x_ref, prev_ref, taps_ref, cols_ref, arow_ref, skip_ref, g_ref, bt_ref, c_ref, y_ref, seq, xs):
    tokens, lanes = x_ref.shape
    nblocks = tokens // BLOCK
    width = lanes // GROUP
    pair = 2 * width
    taps = taps_ref.shape[0]
    seq[0:8, :] = prev_ref[...]
    for k in range(nblocks):
        seq[8 + k * BLOCK : 8 + (k + 1) * BLOCK, :] = x_ref[
            k * BLOCK : (k + 1) * BLOCK, :
        ].astype(jnp.float32)
    for k in range(nblocks):
        base = 8 - (taps - 1) + k * BLOCK
        total = taps_ref[0:1, :].astype(jnp.float32) * seq[base : base + BLOCK, :]
        for j in range(1, taps):
            total = total + taps_ref[j : j + 1, :].astype(jnp.float32) * seq[
                base + j : base + j + BLOCK, :
            ]
        xs[k * BLOCK : (k + 1) * BLOCK, :] = silu(total).astype(jnp.bfloat16)
    lane = lax.broadcasted_iota(jnp.int32, (BLOCK, pair), 1)
    causal = lax.broadcasted_iota(jnp.int32, (BLOCK, BLOCK), 0) >= lax.broadcasted_iota(
        jnp.int32, (BLOCK, BLOCK), 1
    )
    for p in range(GROUP // 2):
        here = slice(p * pair, (p + 1) * pair)
        head = 2 * p
        state = None
        for k in range(nblocks):
            rows = slice(k * BLOCK, (k + 1) * BLOCK)
            x2 = xs[rows, here]
            left, right, cum = spread(cols_ref, 0, head, rows, lane, width)
            weights = []
            for i, col in ((0, left), (1, right)):
                diff = col - arow_ref[head + i : head + i + 1, rows]
                decay = jnp.exp2(jnp.where(causal, diff, NEG))
                weights.append((decay * g_ref[rows, :]).astype(jnp.bfloat16))
            zero = jnp.zeros_like(x2)
            both = jnp.concatenate(
                [jnp.where(lane < width, x2, zero), jnp.where(lane < width, zero, x2)], axis=0
            )
            out = dot(jnp.concatenate(weights, axis=1), both)
            x2f = x2.astype(jnp.float32)
            out = out + skip_ref[:, here] * x2f
            if k > 0:
                out = out + jnp.exp2(cum) * dot(c_ref[rows, :], state.astype(jnp.bfloat16))
            y_ref[rows, here] = out
            if k < nblocks - 1:
                _, _, acol = spread(cols_ref, GROUP, head, rows, lane, width)
                end = cum[BLOCK - 1 : BLOCK, :]
                scaled = (x2f * jnp.exp2(end - acol)).astype(jnp.bfloat16)
                update = dot(bt_ref[:, rows], scaled)
                state = update if k == 0 else jnp.exp2(end) * state + update


def scan_call(x_in, prev, taps, cols, arow, skip, g, bt, c):
    tokens, channels = x_in.shape
    groups = cols.shape[0]
    lanes = channels // groups
    n = c.shape[1]
    return pl.pallas_call(
        scan_kernel,
        grid=(groups,),
        in_specs=[
            pl.BlockSpec((tokens, lanes), lambda i: (0, i)),
            pl.BlockSpec((8, lanes), lambda i: (0, i)),
            pl.BlockSpec((taps.shape[0], lanes), lambda i: (0, i)),
            pl.BlockSpec((None, tokens, 2 * GROUP), lambda i: (i, 0, 0)),
            pl.BlockSpec((GROUP, tokens), lambda i: (i, 0)),
            pl.BlockSpec((1, lanes), lambda i: (0, i)),
            pl.BlockSpec((tokens, BLOCK), lambda i: (0, 0)),
            pl.BlockSpec((n, tokens), lambda i: (0, 0)),
            pl.BlockSpec((tokens, n), lambda i: (0, 0)),
        ],
        out_specs=pl.BlockSpec((tokens, lanes), lambda i: (0, i)),
        out_shape=jax.ShapeDtypeStruct((tokens, channels), jnp.float32),
        scratch_shapes=[
            pltpu.VMEM((tokens + 8, lanes), jnp.float32),
            pltpu.VMEM((tokens, lanes), jnp.bfloat16),
        ],
        compiler_params=pltpu.CompilerParams(vmem_limit_bytes=VMEM),
        cost_estimate=QUICK,
        name="scan_blocks",
    )(x_in, prev, taps, cols, arow, skip, g, bt, c)


def gate_kernel(y_ref, z_ref, cols_ref, h_ref, c_ref, gain_ref, out_ref, sq_ref):
    tokens, lanes = y_ref.shape
    nblocks = tokens // BLOCK
    width = lanes // GROUP
    pair = 2 * width
    lane = lax.broadcasted_iota(jnp.int32, (BLOCK, pair), 1)

    @pl.when(pl.program_id(0) == 0)
    def _():
        sq_ref[...] = jnp.zeros_like(sq_ref)

    for k in range(nblocks):
        rows = slice(k * BLOCK, (k + 1) * BLOCK)
        read = lax.dot_general(
            c_ref[rows, :], h_ref[...], (((1,), (1,)), ((), ())), preferred_element_type=jnp.float32
        )
        total = sq_ref[rows, :]
        for p in range(GROUP // 2):
            here = slice(p * pair, (p + 1) * pair)
            _, _, cum = spread(cols_ref, 0, 2 * p, rows, lane, width)
            out = y_ref[rows, here] + jnp.exp2(cum) * read[:, here]
            gated = out * silu(z_ref[rows, here].astype(jnp.float32))
            total = total + gated * gated
            out_ref[rows, here] = (gated * gain_ref[:, here]).astype(jnp.bfloat16)
        sq_ref[rows, :] = total


def gate_call(y, z, cols, h, c, gain):
    tokens, channels = y.shape
    groups = cols.shape[0]
    lanes = channels // groups
    n = c.shape[1]
    return pl.pallas_call(
        gate_kernel,
        grid=(groups,),
        in_specs=[
            pl.BlockSpec((tokens, lanes), lambda i: (0, i)),
            pl.BlockSpec((tokens, lanes), lambda i: (0, i)),
            pl.BlockSpec((None, tokens, GROUP), lambda i: (i, 0, 0)),
            pl.BlockSpec((lanes, n), lambda i: (i, 0)),
            pl.BlockSpec((tokens, n), lambda i: (0, 0)),
            pl.BlockSpec((1, lanes), lambda i: (0, i)),
        ],
        out_specs=[
            pl.BlockSpec((tokens, lanes), lambda i: (0, i)),
            pl.BlockSpec((tokens, 128), lambda i: (0, 0)),
        ],
        out_shape=[
            jax.ShapeDtypeStruct((tokens, channels), jnp.bfloat16),
            jax.ShapeDtypeStruct((tokens, 128), jnp.float32),
        ],
        compiler_params=pltpu.CompilerParams(vmem_limit_bytes=VMEM),
        cost_estimate=QUICK,
        name="gate_blocks",
    )(y, z, cols, h, c, gain)


def project_kernel(cuts, rows_ref, mine_ref, value_ref, *refs):
    pieces, out_ref, value, held, total, sems = refs[:-5], *refs[-5:]
    depth = value.shape[1] // 2
    loads = []
    for half in range(2):
        span = slice(half * depth, (half + 1) * depth)
        whole = pltpu.make_async_copy(
            value_ref.at[:, span], value.at[:, span], sems.at[half, len(cuts)]
        )
        whole.start()
        copies = []
        for i, (piece, first, size) in enumerate(cuts):
            at = pl.multiple_of(rows_ref[i], 16)
            copy = pltpu.make_async_copy(
                pieces[piece].at[pl.ds(first, size), span],
                held.at[pl.ds(at, size), span],
                sems.at[half, i],
            )
            pl.when(mine_ref[i] == 1)(copy.start)
            copies.append(copy)
        loads.append((span, whole, copies))
    step = 256
    for half, (span, whole, copies) in enumerate(loads):
        whole.wait()
        for i, copy in enumerate(copies):
            pl.when(mine_ref[i] == 1)(copy.wait)
        for at in range(0, out_ref.shape[1], step):
            cols = slice(at, min(at + step, out_ref.shape[1]))
            part = lax.dot_general(
                value[:, span],
                held[cols, span],
                (((1,), (1,)), ((), ())),
                preferred_element_type=jnp.float32,
            )
            if half == 0:
                total[:, cols] = part
            else:
                out_ref[:, cols] = (total[:, cols] + part).astype(out_ref.dtype)


def project(value, pieces, cuts, rows, mine, total, dtype):
    tokens, channels = value.shape
    return pl.pallas_call(
        functools.partial(project_kernel, cuts),
        in_specs=[pl.BlockSpec(memory_space=pltpu.SMEM)] * 2
        + [pl.BlockSpec(memory_space=pl.ANY)] * (1 + len(pieces)),
        out_specs=pl.BlockSpec(memory_space=pltpu.VMEM),
        out_shape=jax.ShapeDtypeStruct((tokens, total), dtype),
        scratch_shapes=[
            pltpu.VMEM((tokens, channels), value.dtype),
            pltpu.VMEM((total, channels), pieces[0].dtype),
            pltpu.VMEM((tokens, total), jnp.float32),
            pltpu.SemaphoreType.DMA((2, len(cuts) + 1)),
        ],
        compiler_params=pltpu.CompilerParams(vmem_limit_bytes=60 * 2**20),
        cost_estimate=QUICK,
        name="project_rows",
    )(rows, mine, value, *pieces)


def choose_kernel(rows_ref, states_ref, out_ref, sems):
    copies = [
        pltpu.make_async_copy(states_ref.at[rows_ref[j]], out_ref.at[j], sems.at[j])
        for j in range(out_ref.shape[0])
    ]
    for copy in copies:
        copy.start()
    for copy in copies:
        copy.wait()


def choose(rows, states):
    count = rows.shape[0]
    return pl.pallas_call(
        choose_kernel,
        in_specs=[
            pl.BlockSpec(memory_space=pltpu.SMEM),
            pl.BlockSpec(memory_space=pl.ANY),
        ],
        out_specs=pl.BlockSpec(memory_space=pl.ANY),
        out_shape=jax.ShapeDtypeStruct((count, *states.shape[1:]), states.dtype),
        scratch_shapes=[pltpu.SemaphoreType.DMA((count,))],
        compiler_params=pltpu.CompilerParams(vmem_limit_bytes=16 * 2**20),
        cost_estimate=QUICK,
        name="choose_rows",
    )(rows, states)


def gather_step(held, axis, step):
    n = lax.axis_size(axis)
    low = (lax.axis_index(axis) & step) == 0
    other = lax.ppermute(held, axis, [(i, i ^ step) for i in range(n)])
    return jnp.concatenate([jnp.where(low, held, other), jnp.where(low, other, held)], axis=0)


def gather_rows(block):
    n = lax.axis_size("cache")
    me = lax.axis_index("cache")
    rows = block.shape[0]
    spot = me // 2
    share = rows * 2 // 5
    if not (n == 8 and lax.axis_size("groups") == 2 and share % 16 == 0 and rows % 16 == 0):
        for _ in range(2):
            yield ()
        every = lax.all_gather(block, "cache", axis=0)
        yield [every[i] for i in range(n)], [(i, 0, rows, i, 0) for i in range(n)]
        return

    def swap(value, pairs):
        return lax.ppermute(
            value, "cache", [(2 * i + p, 2 * j + p) for i, j in pairs for p in (0, 1)]
        )

    def across(value):
        return lax.ppermute(value[:share], "groups", [(0, 1), (1, 0)])

    def beside(value):
        return lax.ppermute(value, "cache", [(i, i ^ 1) for i in range(n)])

    tie = lambda *values: lax.optimization_barrier(values)
    side = lax.axis_index("groups")
    inner = (spot == 1) | (spot == 2)
    own = jnp.concatenate(
        [lax.dynamic_slice_in_dim(block, side * share, share, 0), block[2 * share :]], axis=0
    )
    pairs = [(0, 1), (1, 0), (2, 3), (3, 2)]
    middle = [(1, 2), (2, 1)]
    outward = [(1, 0), (2, 3)]
    own_y, mate, far = beside(own), swap(own, pairs), swap(own, middle)
    own_y, mate, far = yield own_y, mate, far
    end, far_out, mate_y = swap(mate, middle), swap(far, outward), beside(mate)
    own_yx, mate_x = across(own_y), across(mate)
    end, far_out, mate_y, own_yx = tie(end, far_out, mate_y, own_yx)
    far = jnp.where(inner, far, far_out)
    end_out, far_y = swap(end, outward), beside(far)
    mate_yx, far_x = across(mate_y), across(far)
    end_out, far_y, mate_x, mate_yx, far_x = yield end_out, far_y, mate_x, mate_yx, far_x
    end = jnp.where(inner, end, end_out)
    end_y = beside(end)
    end_x = across(end)
    end_yx = beside(end_x)
    far_y, end_x = tie(far_y, end_x)
    far_yx = across(far_y)

    z_far, z_end = jnp.where(spot < 2, 2, 1), jnp.where(spot < 2, 3, 0)
    odd = me % 2
    pieces, cuts = [block], [(0, 0, rows, me, 0)]
    for index, plain, other in (
        (me ^ 1, own_y, own_yx),
        (me ^ 2, mate, mate_x),
        (me ^ 3, mate_y, mate_yx),
        (2 * z_far + odd, far, far_x),
        (2 * z_far + 1 - odd, far_y, far_yx),
        (2 * z_end + odd, end, end_x),
        (2 * z_end + 1 - odd, end_y, end_yx),
    ):
        at = len(pieces)
        pieces += [plain, other]
        cuts += [
            (at, 0, share, index, side * share),
            (at, share, rows - 2 * share, index, 2 * share),
            (at + 1, 0, share, index, (1 - side) * share),
        ]
    yield pieces, cuts


def body(
    x_in,
    z_in,
    bc_in,
    dt_in,
    conv_x,
    conv_bc,
    a_log,
    dt_bias,
    d_skip,
    norm_gain,
    out_weight,
    store_ssm,
    stored_conv_inputs,
    store_convbc,
    hits,
    assign,
    lengths,
):
    ncache = lax.axis_size("cache")
    requests = hits.shape[0]
    local_slots, heads, width, n = store_ssm.shape
    taps_prev = stored_conv_inputs.shape[1]
    tokens, channels = x_in.shape
    nblocks = tokens // BLOCK
    groups = heads // GROUP

    row_of = hits[:, 0] * local_slots + hits[:, 1]
    position_hits = (assign[:, None] == jnp.arange(requests)[None, :]).astype(jnp.int32)
    row_at = jnp.sum(position_hits * row_of[None, :], axis=1)
    row_here = row_at[lax.axis_index("cache")]

    def tie(*values):
        return lax.optimization_barrier(values)

    small = jnp.concatenate([stored_conv_inputs, store_convbc], axis=2)
    small = gather_step(small.reshape(1, -1, 128), "cache", 1)
    small, out_weight = tie(small, out_weight)
    size = 2
    while 2 * size < ncache:
        small = gather_step(small, "cache", size)
        size *= 2
    gathered = gather_rows(out_weight)
    *step, store_ssm, small = tie(*next(gathered), store_ssm, small)
    small = gather_step(small, "cache", size)
    step = gathered.send(tuple(step))

    share = channels // ncache
    states = store_ssm.astype(jnp.bfloat16).reshape(local_slots, ncache, share, n)
    states = states.transpose(1, 0, 2, 3)
    states, small = tie(states, small)
    states = lax.all_to_all(states, "cache", split_axis=0, concat_axis=0, tiled=True)
    chosen = choose(row_at.astype(jnp.int32), states.reshape(ncache * local_slots, share, n))

    small = lax.dynamic_index_in_dim(
        small.reshape(ncache * local_slots, taps_prev, -1), row_here, 0, keepdims=False
    )
    prev_x = jnp.concatenate(
        [jnp.zeros((8 - taps_prev, channels), jnp.float32), small[:, :channels]], axis=0
    )

    bcs = conv_silu(small[:, channels:], bc_in, conv_bc)
    b = bcs[:, :n]
    c = bcs[:, n:]
    step_size = jax.nn.softplus(dt_in + dt_bias[None, :])
    rate = step_size * (-LOG2E * jnp.exp(a_log))[None, :]
    b3 = b.reshape(nblocks, BLOCK, n)
    c3 = c.reshape(nblocks, BLOCK, n)
    g = jnp.einsum("ktn,ksn->kts", c3, b3, preferred_element_type=jnp.float32)
    causal = jnp.arange(BLOCK)[:, None] >= jnp.arange(BLOCK)[None, :]
    g = jnp.where(causal[None], g, 0.0).reshape(tokens, BLOCK)
    cum = jnp.einsum(
        "ts,ksh->kth",
        causal.astype(jnp.float32),
        rate.reshape(nblocks, BLOCK, heads),
        precision=lax.Precision.HIGHEST,
    )
    ends = cum[:, -1, :]
    before = jnp.concatenate([jnp.zeros((1, heads), jnp.float32), jnp.cumsum(ends, axis=0)[:-1]])
    whole = (cum + before[:, None, :]).reshape(tokens, heads)
    cum = cum.reshape(tokens, heads)
    acol = cum - jnp.log2(step_size)

    def grouped(v):
        return v.reshape(tokens, groups, GROUP).transpose(1, 0, 2)

    cols = jnp.concatenate([grouped(cum), grouped(acol)], axis=2)
    skip = jnp.repeat(d_skip, width)[None, :]
    y = scan_call(x_in, prev_x, conv_x, cols, acol.T, skip, g, b.T, c)
    whole = grouped(whole)
    gain = norm_gain[None, :]
    cores = [(0, 1), (1, 0)]
    core = lax.axis_index("tensor")
    start = lax.all_to_all(chosen, "cache", split_axis=0, concat_axis=0, tiled=True)
    start = start.reshape(channels, n)
    *step, y = tie(*step, y)
    pieces, cuts = gathered.send(tuple(step))
    gated, squares = gate_call(y, z_in, whole, start, c, gain)
    squares = jnp.sum(squares, axis=1)
    squares = squares + lax.ppermute(squares, "tensor", cores)
    valid = jnp.arange(tokens) < lengths[0]
    scale = jnp.where(valid, lax.rsqrt(squares / INNER + 1e-05), 0.0)[:, None]

    half = ncache // 2
    rows = out_weight.shape[0]
    places = jnp.stack(
        [lax.rem(jnp.int32(index), half) * rows + row for _, _, _, index, row in cuts]
    )
    owners = jnp.stack([jnp.int32(index) // half for _, _, _, index, _ in cuts])
    cuts = tuple(cut[:3] for cut in cuts)

    def products(owner, dtype):
        mine = (owners == owner).astype(jnp.int32)
        return project(gated, pieces, cuts, places.astype(jnp.int32), mine, half * rows, dtype)

    other = lax.ppermute(products(1 - core, jnp.bfloat16), "tensor", cores)
    summed = products(core, jnp.bfloat16).astype(jnp.float32) + other.astype(jnp.float32)
    return (summed * scale).astype(jnp.bfloat16)


def solution(mesh):
    return jax.shard_map(
        body,
        mesh=mesh,
        in_specs=(
            P(("groups", "cache"), "tensor"),
            P(("groups", "cache"), "tensor"),
            P(("groups", "cache"), None),
            P(("groups", "cache"), "tensor"),
            P(None, "tensor"),
            P(),
            P("tensor"),
            P("tensor"),
            P("tensor"),
            P("tensor"),
            P("cache", "tensor"),
            P(("groups", "cache"), "tensor", None, None),
            P(("groups", "cache"), None, "tensor"),
            P(("groups", "cache"), None, None),
            P("groups", None),
            P("groups"),
            P(("groups", "cache")),
        ),
        out_specs=P(("groups", "cache"), "tensor"),
        check_vma=False,
    )
```
